32 devices in a mesh: grp: 2 (over y), row: 4 (over z), mic: 2 (over x), orient: 2 (over core).
Axes of the slice: x: 2, y: 2, z: 4, core: 2. Of those that a mesh axis runs over, the one named last changes fastest.
Arguments:
- spectra: bfloat16 [8, 2, 2048, 2048], P(('grp', 'mic'), None, 'row'), parts along dimension 0, may hold values from -6 to 6
- bank: bfloat16 [8, 384, 384], replicated, as said below
- orient_index: int32 [16], P('grp'), parts along dimension 0, may hold values from 0 to 7, as said below
Outputs:
- peak_map: float32 [8, 4, 512, 128], P(('grp', 'mic'), 'row'), parts along dimension 0
- power_map: float32 [8, 4, 512, 128], P(('grp', 'mic'), 'row'), parts along dimension 0
The draws below stay inside these ranges and needn't reach their ends.
There are 2 independent parts, one for each index of `grp`. The reference program is written for one: setup_inputs(seed, part) draws one part's arguments, and reference() takes and returns one part's arrays. A program takes and returns all parts, laid end to end along the dimension named above; an argument that names none is the same for every part. Nothing has to cross between parts.
Inputs may be any that keep to these rules, and one draw needn't show every extreme that they name: `bank`: projection images of the table. `orient_index`: each entry names one projection of the table; entries may repeat.
All inputs are finite; a program needn't handle non-finite values.
Results may differ from the reference program's by a relative error of at most 0.0051.
Values may be sent and summed in bfloat16 or wider, within the bound.
No kernel may reach another device: no remote copies, remote signals or barrier semaphores. Data moves between devices by JAX's collectives and lax.ppermute only.
A program may use at most 128 MiB of HBM per device.

```python
import math
import jax
import jax.numpy as jnp
import numpy as np
from jax import lax

NFFT = 2048
TSIZE = 384
WCOLS = 128
WIN = 8
BANK = 8
MICS = 4
RBANDS = 4
YB = 512


def draw_bank(key, part):
    key_rows = jax.random.fold_in(key, 101)
    key_cols = jax.random.fold_in(key, 202)
    key_noise = jax.random.fold_in(key, 303)
    key_shift = jax.random.fold_in(key, 404)
    row_scale = jnp.exp(jax.random.uniform(key_rows, (BANK, TSIZE, 1), jnp.float32) * math.log(10.0))
    col_scale = jnp.exp(jax.random.uniform(key_cols, (BANK, 1, TSIZE), jnp.float32) * math.log(10.0))
    noise = jax.random.normal(key_noise, (BANK, TSIZE, TSIZE), jnp.float32)
    offset = jax.random.normal(key_shift, (BANK, 1, 1), jnp.float32)
    values = noise * row_scale * col_scale + 3.0 * offset
    return values.astype(jnp.bfloat16)


def draw_orient_index(key, part):
    key_values = jax.random.fold_in(key, 505)
    key_order = jax.random.fold_in(key, 606)
    values = jax.random.randint(key_values, (WIN,), 0, BANK, dtype=jnp.int32)
    order = jax.random.permutation(key_order, WIN)
    positions = jnp.arange(WIN, dtype=jnp.int32)
    values = jnp.where(positions == order[0], BANK - 1, values)
    values = jnp.where(positions == order[1], 0, values)
    return values.astype(jnp.int32)


def block_levels(own_key, shape, pieces, low, top_value):
    level = 1.0
    for dim, shards_of in pieces:
        heights = jax.random.uniform(jax.random.fold_in(jax.random.fold_in(own_key, 6), dim), (shards_of,), jnp.float32, low / len(pieces), top_value / len(pieces))
        level = level * jnp.repeat(jnp.exp(heights), shape[dim] // shards_of).reshape((-1,) + (1,) * (len(shape) - 1 - dim))
    return level


def bell_draw(key, shape, scale, reach, cuts=(), kind=jnp.bfloat16):
    values = jax.random.normal(key, shape, jnp.float32) * scale
    if len(cuts) > 0:
        values = block_levels(key, shape, cuts, -0.22, 0.18) * values
    return jnp.clip(values, min=-reach, max=reach).astype(kind)


def setup_inputs(seed: int = 0, part: int = 0) -> dict:
    keys = jax.random.split(jax.random.key(seed), 4)
    part_keys = jax.random.split(jax.random.fold_in(keys[3], part), 4)
    return {
        "spectra": bell_draw(part_keys[0], (MICS, 2, NFFT, NFFT), 1.0, 6.0, ((0, 2), (2, 4))),
        "bank": draw_bank(jax.random.fold_in(keys[3], 71), part),
        "orient_index": draw_orient_index(jax.random.fold_in(jax.random.fold_in(keys[3], part), 71), part),
    }


two_pi = 2.0 * math.pi

def phase_table(row_start, row_count, col_start, col_count, period):
    row_ids = row_start + jnp.arange(row_count, dtype=jnp.int32)
    col_ids = col_start + jnp.arange(col_count, dtype=jnp.int32)
    wrapped = row_ids[:, None] * col_ids[None, :] % period
    angles = wrapped.astype(jnp.float32) * (two_pi / period)
    return (jnp.cos(angles), jnp.sin(angles))

def normalize(picture):
    values = picture.astype(jnp.float32)
    centred = values - jnp.mean(values)
    factor = lax.rsqrt(jnp.mean(centred * centred) + 1e-06)
    return (centred * factor).astype(jnp.bfloat16)

def reverse_bits(number, digits):
    result = number * 0
    for digit in range(digits):
        result = result + number // (1 << digit) % 2 * (1 << digits - 1 - digit)
    return result

def reference(spectra, bank, orient_index):
    sections = RBANDS.bit_length() - 1
    templates = jax.vmap(normalize)(bank[orient_index])
    cos_y, sin_y = phase_table(0, NFFT, 0, TSIZE, NFFT)
    cos_x, sin_x = phase_table(0, TSIZE, 0, NFFT, NFFT)
    cos_e, sin_e = phase_table(0, NFFT, 0, WCOLS, NFFT)
    cos_y = cos_y.astype(jnp.bfloat16)
    neg_sin_y = -sin_y.astype(jnp.bfloat16)
    cos_x = cos_x.astype(jnp.bfloat16)
    sin_x = sin_x.astype(jnp.bfloat16)
    cos_e = cos_e.astype(jnp.bfloat16)
    sin_e = sin_e.astype(jnp.bfloat16)
    cos_c, sin_c = phase_table(0, NFFT, 0, NFFT, NFFT)
    factor = 1.0 / (NFFT * TSIZE)

    def one_orientation(template):
        pass_re = jnp.dot(cos_y, template, preferred_element_type=jnp.float32).astype(jnp.bfloat16)
        pass_im = jnp.dot(neg_sin_y, template, preferred_element_type=jnp.float32).astype(jnp.bfloat16)
        spec_re = (jnp.dot(pass_re, cos_x, preferred_element_type=jnp.float32) + jnp.dot(pass_im, sin_x, preferred_element_type=jnp.float32)).astype(jnp.bfloat16)
        spec_im = (jnp.dot(pass_im, cos_x, preferred_element_type=jnp.float32) - jnp.dot(pass_re, sin_x, preferred_element_type=jnp.float32)).astype(jnp.bfloat16)
        tmpl_re = spec_re.astype(jnp.float32)
        tmpl_im = spec_im.astype(jnp.float32)

        def one_micrograph(spectrum):
            mic_re = spectrum[0].astype(jnp.float32)
            mic_im = spectrum[1].astype(jnp.float32)
            prod_re = (mic_re * tmpl_re + mic_im * tmpl_im).astype(jnp.bfloat16)
            prod_im = (mic_im * tmpl_re - mic_re * tmpl_im).astype(jnp.bfloat16)
            part_re = jnp.dot(prod_re, cos_e, preferred_element_type=jnp.float32) - jnp.dot(prod_im, sin_e, preferred_element_type=jnp.float32)
            part_im = jnp.dot(prod_re, sin_e, preferred_element_type=jnp.float32) + jnp.dot(prod_im, cos_e, preferred_element_type=jnp.float32)
            column = jnp.dot(cos_c, part_re, precision=lax.Precision.HIGHEST) - jnp.dot(sin_c, part_im, precision=lax.Precision.HIGHEST)
            return column * factor
        return lax.map(one_micrograph, spectra)

    def accumulate(carry, template):
        corr = one_orientation(template)
        return ((jnp.maximum(carry[0], corr), carry[1] + corr * corr), None)
    start_peak = jnp.full((MICS, NFFT, WCOLS), -1e+30, jnp.float32)
    start_power = jnp.zeros((MICS, NFFT, WCOLS), jnp.float32)
    totals, unused = lax.scan(accumulate, (start_peak, start_power), templates)
    reversal = np.array([reverse_bits(place, sections) for place in range(RBANDS)], dtype=np.int32)

    def arrange(field):
        shaped = field.reshape(MICS, YB, RBANDS, WCOLS).transpose(0, 2, 1, 3)
        return shaped[:, reversal]
    return (arrange(totals[0]), arrange(totals[1]))
```

```python
import functools
import math

import jax
import jax.numpy as jnp
import ml_dtypes
import numpy as np
from jax import lax
from jax.experimental import pallas as pl
from jax.experimental.pallas import tpu as pltpu
from jax.sharding import PartitionSpec as P

WCOLS = 128
PAD = 16

two_pi = 2.0 * math.pi
BF16 = ml_dtypes.bfloat16
PARAMS = pltpu.CompilerParams(vmem_limit_bytes=40 * 1024 * 1024)


def bits(count):
    return count.bit_length() - 1


def reverse_bits(number, digits):
    result = number * 0
    for digit in range(digits):
        result = result + number // (1 << digit) % 2 * (1 << digits - 1 - digit)
    return result


def phases(rows, cols, period):
    angles = np.outer(rows, cols) % period * (two_pi / period)
    return np.cos(angles), np.sin(angles)


def window_table(length, win, mirrored):
    ratio = length // win
    lanes = win // ratio
    sign = 1 if mirrored else -1
    base = np.arange(win)[:, None] + sign * ratio * np.arange(lanes)[None, :]
    d = (length // ratio * np.arange(ratio)[:, None, None] + base[None]) % length
    u = np.arange(win)
    kernel = np.exp(2j * np.pi * (np.outer(np.arange(length), u) % length) / length).sum(1) / win
    val = kernel[d]
    upper = np.concatenate([val.real, -sign * val.imag], 2)
    lower = np.concatenate([-val.imag, -sign * val.real], 2)
    return np.concatenate([upper, lower], 1).astype(BF16)


def tiles_of(re, im, lanes, axis):
    pieces = []
    for start in range(0, re.shape[axis], lanes):
        cut = [slice(None)] * re.ndim
        cut[axis] = slice(start, start + lanes)
        pieces += [re[tuple(cut)], im[tuple(cut)]]
    return np.concatenate(pieces, axis)


def template_table(tsize, win, lanes):
    cos, sin = phases(np.arange(tsize), np.arange(win), win)
    upper = tiles_of(cos, -sin, lanes, 1)
    lower = tiles_of(sin, cos, lanes, 1)
    return np.concatenate([upper, lower], 0).astype(BF16)


def back_table(win, lanes):
    cos, sin = phases(np.arange(win), np.arange(WCOLS), win)
    re_rows = np.concatenate([cos, sin], 1)
    im_rows = np.concatenate([-sin, cos], 1)
    return tiles_of(re_rows, im_rows, lanes, 0).astype(BF16)


def column_table(length, classes, cores, band):
    steps = length // classes
    out = []
    for rho in range(classes):
        per_core = []
        for core in range(cores):
            cos, sin = phases(rho + classes * np.arange(steps), core * band + np.arange(band), length)
            per_core.append(np.concatenate([cos, -sin], 1))
        out.append(np.stack(per_core))
    return np.stack(out).astype(BF16)


def flip_table(band):
    out = np.zeros((band + PAD, band), np.float32)
    out[band - np.arange(band), np.arange(band)] = 1.0
    return out.astype(BF16)


def window_kernel(mirrored, place_ref, spec_ref, table_ref, out_ref, acc_ref):
    ratio = table_ref.shape[0]
    win = table_ref.shape[1] // 2
    width = table_ref.shape[2]
    step = pl.program_id(0)

    @pl.when(step == 0)
    def _():
        acc_ref[...] = jnp.zeros_like(acc_ref)

    for part in range(ratio):
        block = lax.rem(step + (part if mirrored else ratio - part), ratio)
        got = jnp.dot(spec_ref[0, 0], table_ref[block, :win], preferred_element_type=jnp.float32)
        got += jnp.dot(spec_ref[0, 1], table_ref[block, win:], preferred_element_type=jnp.float32)
        acc_ref[:, part * width : (part + 1) * width] += got

    @pl.when(step == ratio - 1)
    def _():
        out_ref[...] = acc_ref[...].astype(out_ref.dtype)


def windowed(spectra, table, place, band, dtype, mirrored):
    ratio, double_win, width = table.shape
    win = double_win // 2
    return pl.pallas_call(
        functools.partial(window_kernel, mirrored),
        out_shape=jax.ShapeDtypeStruct((band, ratio * width), dtype),
        grid_spec=pltpu.PrefetchScalarGridSpec(
            num_scalar_prefetch=1,
            grid=(ratio,),
            in_specs=[
                pl.BlockSpec((1, 2, band, win), lambda a, place: (place[0], 0, place[1], a)),
                pl.BlockSpec(table.shape, lambda a, place: (0, 0, 0)),
            ],
            out_specs=pl.BlockSpec((band, ratio * width), lambda a, place: (0, 0)),
            scratch_shapes=[pltpu.VMEM((band, ratio * width), jnp.float32)],
        ),
        compiler_params=PARAMS,
        cost_estimate=pl.CostEstimate(
            flops=2 * band * 2 * win * ratio * ratio * width,
            bytes_accessed=2 * (2 * band * win * ratio + table.size),
            transcendentals=0,
        ),
        name="windowed",
    )(place, spectra, table)


def partial_kernel(members, place_ref, keep_ref, other_ref, flip_ref, tspec_ref, back_ref, *rest):
    outs = rest[:members]
    held_ref, part_ref = rest[members:]
    orient = pl.program_id(0)
    window = part_ref.shape[0]
    band = keep_ref.shape[0]
    rows, width = held_ref.shape
    lanes = 128
    blocks = width // (2 * lanes)

    @pl.when(orient == 0)
    def _():
        held_ref[...] = jnp.dot(flip_ref[...], other_ref[...], preferred_element_type=jnp.float32)
        held_ref[:band] += keep_ref[...]

    total = jnp.zeros((rows, 2 * WCOLS), jnp.float32)
    for block in range(blocks):
        re_at = slice(2 * block * lanes, (2 * block + 1) * lanes)
        im_at = slice((2 * block + 1) * lanes, (2 * block + 2) * lanes)
        mic_re = held_ref[:, re_at]
        mic_im = held_ref[:, im_at]
        tmpl_re = tspec_ref[0, :, re_at].astype(jnp.float32)
        tmpl_im = tspec_ref[0, :, im_at].astype(jnp.float32)
        prod_re = (mic_re * tmpl_re + mic_im * tmpl_im).astype(jnp.bfloat16)
        prod_im = (mic_im * tmpl_re - mic_re * tmpl_im).astype(jnp.bfloat16)
        total += jnp.dot(
            jnp.concatenate([prod_re, prod_im], 1),
            back_ref[2 * block * lanes : (2 * block + 2) * lanes],
            preferred_element_type=jnp.float32,
        )
    part_ref[orient] = total

    @pl.when(orient == window - 1)
    def _():
        group = WCOLS // members
        lane_group = lax.broadcasted_iota(jnp.int32, (rows, WCOLS), 1) // group
        tiles = max(1, window // members)
        mine = place_ref[0]
        for tile in range(tiles):
            for plane in range(2):
                at = slice(plane * WCOLS, (plane + 1) * WCOLS)
                pieces = []
                for i in range(members):
                    piece = part_ref[(tile * members + i) % window, :, at]
                    pieces.append(pltpu.roll(piece, group * i, 1) if i else piece)
                for s in range(members):
                    target = lax.bitwise_xor(mine, s)
                    packed = pieces[0]
                    for i in range(1, members):
                        inside = (lane_group + (members - i)) % members == target
                        packed = jnp.where(inside, pieces[i], packed)
                    start = (plane * tiles + tile) * WCOLS
                    outs[s][:, start : start + WCOLS] = packed.astype(outs[s].dtype)


def partials(keep, other, flip, tspec, back, place, members):
    window, rows, width = tspec.shape
    tiles = max(1, window // members)
    whole = lambda shape: pl.BlockSpec(shape, lambda o, place: (0,) * len(shape))
    out_shape = (rows, 2 * tiles * WCOLS)
    return pl.pallas_call(
        functools.partial(partial_kernel, members),
        out_shape=[jax.ShapeDtypeStruct(out_shape, jnp.bfloat16)] * members,
        grid_spec=pltpu.PrefetchScalarGridSpec(
            num_scalar_prefetch=1,
            grid=(window,),
            in_specs=[
                whole(keep.shape),
                whole(other.shape),
                whole(flip.shape),
                pl.BlockSpec((1, rows, width), lambda o, place: (o, 0, 0)),
                whole(back.shape),
            ],
            out_specs=[whole(out_shape)] * members,
            scratch_shapes=[
                pltpu.VMEM((rows, width), jnp.float32),
                pltpu.VMEM((window, rows, 2 * WCOLS), jnp.float32),
            ],
        ),
        compiler_params=PARAMS,
        cost_estimate=pl.CostEstimate(
            flops=2 * window * rows * width * 2 * WCOLS,
            bytes_accessed=2 * tspec.size,
            transcendentals=0,
        ),
        name="partials",
    )(place, keep, other, flip, tspec, back)


def column_kernel(members, classes, scale, place_ref, factor_ref, table_ref, *rest):
    parts = rest[:members]
    outs = rest[members:]
    cores = table_ref.shape[1]
    steps = table_ref.shape[2]
    band = table_ref.shape[3] // 2
    wide = parts[0].shape[1] // 2
    step = pl.program_id(0)
    spread = members // cores
    corr = jnp.zeros((steps, wide), jnp.float32)
    for s_core in range(cores):
        z_re = jnp.zeros((band, wide), jnp.float32)
        z_im = jnp.zeros((band, wide), jnp.float32)
        more_re = jnp.zeros((PAD, wide), jnp.float32)
        more_im = jnp.zeros((PAD, wide), jnp.float32)
        for s_row in range(spread):
            s = s_row * cores + s_core
            cos, sin = factor_ref[step, s, 0], factor_ref[step, s, 1]
            re = parts[s][:band, :wide].astype(jnp.float32)
            im = parts[s][:band, wide:].astype(jnp.float32)
            z_re += cos * re - sin * im
            z_im += sin * re + cos * im
            t = s_row * cores + (s_core ^ 1)
            cos, sin = factor_ref[step, t, 2], factor_ref[step, t, 3]
            re = parts[t][band:, :wide].astype(jnp.float32)
            im = parts[t][band:, wide:].astype(jnp.float32)
            more_re += cos * re - sin * im
            more_im += sin * re + cos * im
        stacked = jnp.concatenate(
            [z_re[:PAD] + more_re, z_re[PAD:], z_im[:PAD] + more_im, z_im[PAD:]], 0
        ).astype(jnp.bfloat16)
        core = lax.bitwise_xor(place_ref[1], s_core)
        corr += jnp.dot(table_ref[0, core], stacked, preferred_element_type=jnp.float32)
    corr = corr * (scale * factor_ref[step, members, 0])
    peak = corr[:, :WCOLS]
    power = corr[:, :WCOLS] * corr[:, :WCOLS]
    for start in range(WCOLS, wide, WCOLS):
        more = corr[:, start : start + WCOLS]
        peak = jnp.maximum(peak, more)
        power = power + more * more
    group = WCOLS // members
    shift = group
    while shift < WCOLS:
        peak = jnp.maximum(peak, pltpu.roll(peak, shift, 1))
        power = power + pltpu.roll(power, shift, 1)
        shift *= 2
    power = power * factor_ref[step, members, 1]
    height = steps // (members // 2)
    lane_group = lax.broadcasted_iota(jnp.int32, (height, WCOLS), 1) // group
    kappa = (lane_group + (members - place_ref[0])) % members
    packed = peak[:height]
    for k in range(1, members):
        source = (power if k % 2 else peak)[k // 2 * height : (k // 2 + 1) * height]
        packed = jnp.where(kappa == k, source, packed)
    for s in range(classes):

        @pl.when(step == s)
        def _():
            outs[s][...] = packed.astype(outs[s].dtype)


def columns(parts, table, place, factor, scale, dtype):
    classes, cores, steps, double_band = table.shape
    members = len(parts)
    height = steps // (members // 2)
    whole = lambda shape: pl.BlockSpec(shape, lambda s, place, factor: (0,) * len(shape))
    return pl.pallas_call(
        functools.partial(column_kernel, members, classes, scale),
        out_shape=[jax.ShapeDtypeStruct((height, WCOLS), dtype)] * classes,
        grid_spec=pltpu.PrefetchScalarGridSpec(
            num_scalar_prefetch=2,
            grid=(classes,),
            in_specs=[
                pl.BlockSpec(
                    (1, cores, steps, double_band), lambda s, place, factor: (place[2 + s], 0, 0, 0)
                )
            ]
            + [whole(part.shape) for part in parts],
            out_specs=[whole((height, WCOLS))] * classes,
        ),
        compiler_params=PARAMS,
        name="columns",
    )(place, factor, table, *parts)


def unpack_kernel(members, classes, place_ref, *rest):
    near = rest[:classes]
    far = rest[classes : 2 * classes]
    peak_ref, power_ref = rest[2 * classes :]
    row, core = place_ref[0], place_ref[1]
    half = classes // 2
    height = near[0].shape[0]
    group = WCOLS // members
    lane_group = lax.broadcasted_iota(jnp.int32, (height, WCOLS), 1) // group
    side = row // half
    for delta in range(2):
        mic = lax.bitwise_xor(side, delta)
        for k in range(members):
            wanted = (lane_group + (members - k)) % members
            value = jnp.zeros((height, WCOLS), jnp.float32)
            for low in range(half):
                s = delta * half + low
                base = lax.bitwise_xor(row, s) % half * 2
                for source, at in ((near, core), (far, 1 - core)):
                    value = jnp.where(wanted == base + at, source[s][...].astype(jnp.float32), value)
            if k:
                value = pltpu.roll(value, WCOLS - k * group, 1)
            target = power_ref if k % 2 else peak_ref
            target[mic, 0, k // 2 * height : (k // 2 + 1) * height, :] = value


def unpack(near, far, place, steps, members):
    classes = len(near)
    shape = jax.ShapeDtypeStruct((2, 1, steps, WCOLS), jnp.float32)
    return pl.pallas_call(
        functools.partial(unpack_kernel, members, classes),
        out_shape=[shape, shape],
        in_specs=[pl.BlockSpec(memory_space=pltpu.SMEM)]
        + [pl.BlockSpec(memory_space=pltpu.VMEM)] * (2 * classes),
        out_specs=[pl.BlockSpec(memory_space=pltpu.VMEM)] * 2,
        compiler_params=PARAMS,
        name="unpack",
    )(place, *near, *far)


def normalize(picture):
    values = picture.astype(jnp.float32)
    centred = values - jnp.mean(values)
    factor = lax.rsqrt(jnp.mean(centred * centred) + 1e-06)
    return (centred * factor).astype(jnp.bfloat16)


def template_spectra(bank, orient_index, band_id, band, length, win, lanes):
    tsize = bank.shape[1]
    templates = jax.vmap(normalize)(bank[orient_index])
    cos, sin = phases(np.arange(length + PAD), np.arange(tsize), length)
    rows = jnp.asarray(np.stack([cos, -sin]).astype(BF16))
    left = lax.dynamic_slice_in_dim(rows, band_id * band, band + PAD, 1)
    rowpass = jnp.einsum("cay,oyx->oacx", left, templates, preferred_element_type=jnp.float32)
    rowpass = rowpass.astype(jnp.bfloat16).reshape(templates.shape[0], band + PAD, 2 * tsize)
    right = jnp.asarray(template_table(tsize, win, lanes))
    spectrum = jnp.einsum("oax,xk->oak", rowpass, right, preferred_element_type=jnp.float32)
    return spectrum.astype(jnp.bfloat16)


def shards(spectra, bank, orient_index):
    length = spectra.shape[3]
    tsize = bank.shape[1]
    classes = lax.axis_size("row")
    cores = lax.axis_size("orient")
    row = lax.axis_index("row")
    core = lax.axis_index("orient")
    count = classes * cores
    members = count // 2
    half = classes // 2
    band = length // count
    steps = length // classes
    win = 1 << (tsize + WCOLS - 2).bit_length()
    lanes = win // (length // win)
    device = row * cores + core
    member = device % members
    side = device // members
    line = ("row", "orient")

    send_place = jnp.stack([1 - side, core]).astype(jnp.int32)
    keep_place = jnp.stack([side, core]).astype(jnp.int32)
    mirror_table = jnp.asarray(window_table(length, win, True))
    sent = windowed(spectra, mirror_table, send_place, band, jnp.bfloat16, True)
    other = lax.ppermute(sent, line, [(i, count - 1 - i) for i in range(count)])
    table = jnp.asarray(window_table(length, win, False))
    keep = windowed(spectra, table, keep_place, band, jnp.float32, False)
    tspec = template_spectra(bank, orient_index, device, band, length, win, lanes)
    parts = partials(
        keep,
        other,
        jnp.asarray(flip_table(band)),
        tspec,
        jnp.asarray(back_table(win, lanes)),
        member[None].astype(jnp.int32),
        members,
    )
    got = [parts[0]]
    for s in range(1, members):
        got.append(lax.ppermute(parts[s], line, [(i, i ^ s) for i in range(count)]))

    step_ids = lax.bitwise_xor(row, jnp.arange(classes, dtype=jnp.int32))
    rho = reverse_bits(step_ids, bits(classes))
    sources = lax.bitwise_xor(member, jnp.arange(members, dtype=jnp.int32))
    roots = np.exp(2j * np.pi * np.arange(classes) / classes)
    root_re = jnp.asarray(np.round(roots.real, 15).astype(np.float32))
    root_im = jnp.asarray(np.round(roots.imag, 15).astype(np.float32))
    own = rho[:, None] * (sources // cores)[None, :] % classes
    after = rho[:, None] * ((sources + 1) // cores)[None, :] % classes
    factor = jnp.stack([root_re[own], root_im[own], root_re[after], root_im[after]], 2)
    sign = 1.0 - 2.0 * (side * rho % 2).astype(jnp.float32)
    window = orient_index.shape[0]
    share = jnp.full_like(sign, window / max(window, members))
    zeros = jnp.zeros_like(sign)
    last = jnp.stack([sign, share, zeros, zeros], 1)[:, None]
    factor = jnp.concatenate([factor, last], 1)
    place = jnp.concatenate([jnp.stack([member, core]), rho]).astype(jnp.int32)
    maps = columns(
        got,
        jnp.asarray(column_table(length, classes, cores, band)),
        place,
        factor,
        1.0 / (length * tsize),
        jnp.float32,
    )
    near = [maps[0]]
    for s in range(1, classes):
        near.append(lax.ppermute(maps[s], "row", [(i, i ^ s) for i in range(classes)]))
    far = [lax.ppermute(m, "orient", [(0, 1), (1, 0)]) for m in near]
    peak, power = unpack(near, far, jnp.stack([row, core]).astype(jnp.int32), steps, members)
    return peak, power


def solution(mesh):
    return jax.shard_map(
        shards,
        mesh=mesh,
        in_specs=(P(("grp", "mic"), None, "row", None), P(), P("grp")),
        out_specs=(P(("grp", "mic"), "row", None, None), P(("grp", "mic"), "row", None, None)),
        check_vma=False,
    )
```

```python
import functools
import math

import jax
import jax.numpy as jnp
import ml_dtypes
import numpy as np
from jax import lax
from jax.experimental import pallas as pl
from jax.experimental.pallas import tpu as pltpu
from jax.sharding import PartitionSpec as P

WCOLS = 128
WINDOW_MB = 57
TEMPLATE_MB = 16
PARTIAL_MB = 16
COLUMN_MB = 12
PAD = 16

two_pi = 2.0 * math.pi
BF16 = ml_dtypes.bfloat16


def params(mebibytes):
    return pltpu.CompilerParams(vmem_limit_bytes=mebibytes * 1024 * 1024)


def bits(count):
    return count.bit_length() - 1


def reverse_bits(number, digits):
    result = number * 0
    for digit in range(digits):
        result = result + number // (1 << digit) % 2 * (1 << digits - 1 - digit)
    return result


def phases(rows, cols, period):
    angles = np.outer(rows, cols) % period * (two_pi / period)
    return np.cos(angles), np.sin(angles)


def window_table(length, win, mirrored):
    ratio = length // win
    lanes = win // ratio
    sign = 1 if mirrored else -1
    base = np.arange(win)[:, None] + sign * ratio * np.arange(lanes)[None, :]
    d = (length // ratio * np.arange(ratio)[:, None, None] + base[None]) % length
    u = np.arange(win)
    kernel = np.exp(2j * np.pi * (np.outer(np.arange(length), u) % length) / length).sum(1) / win
    val = kernel[d]
    return np.concatenate([val.real, val.imag], 2).astype(BF16)


def tiles_of(re, im, lanes, axis):
    pieces = []
    for start in range(0, re.shape[axis], lanes):
        cut = [slice(None)] * re.ndim
        cut[axis] = slice(start, start + lanes)
        pieces += [re[tuple(cut)], im[tuple(cut)]]
    return np.concatenate(pieces, axis)


def template_table(tsize, win, lanes):
    cos, sin = phases(np.arange(tsize), np.arange(win), win)
    upper = tiles_of(cos, -sin, lanes, 1)
    lower = tiles_of(sin, cos, lanes, 1)
    return np.concatenate([upper, lower], 0).astype(BF16)


def split(table):
    upper = table.astype(BF16)
    return np.stack([upper, (table - upper.astype(np.float64)).astype(BF16)])


def back_table(win, lanes):
    cos, sin = phases(np.arange(win), np.arange(WCOLS), win)
    re_rows = np.concatenate([cos, sin], 1)
    im_rows = np.concatenate([-sin, cos], 1)
    table = tiles_of(re_rows, im_rows, lanes, 0)
    return split(table.reshape(win // lanes, 2 * lanes, 2 * WCOLS))


def column_table(length, classes, cores, band):
    steps = length // classes
    freqs = np.arange(cores * band)
    out = []
    for rho in range(classes):
        cos, sin = phases(rho + classes * np.arange(steps), freqs, length)
        out.append(tiles_of(cos, -sin, band, 1))
    return np.stack(out).astype(BF16)


def flip_table(band):
    out = np.zeros((band + PAD, band), np.float32)
    out[band - np.arange(band), np.arange(band)] = 1.0
    return out.astype(BF16)


def vmem(count):
    return [pl.BlockSpec(memory_space=pltpu.VMEM)] * count


def hbm(count):
    return [pl.BlockSpec(memory_space=pltpu.HBM)] * count


SMEM = pl.BlockSpec(memory_space=pltpu.SMEM)


def place():
    row, core = lax.axis_index("row"), lax.axis_index("orient")
    cores = lax.axis_size("orient")
    members = lax.axis_size("row") * cores // 2
    device = row * cores + core
    return row, core, members, device % members, device // members


def window_kernel(mirrored, place_ref, spec_ref, table_ref, out_ref):
    ratio, win, width = table_ref.shape
    lanes = width // 2
    rows = out_ref.shape[0]
    pieces = []
    for step in range(ratio):
        at = slice(step * win, (step + 1) * win)
        pieces += [spec_ref[0, part, :, at] for part in range(2)]
    stacked = jnp.concatenate(pieces, 0)
    got = [
        jnp.dot(stacked, table_ref[which], preferred_element_type=jnp.float32)
        for which in range(ratio)
    ]
    for part in range(ratio):
        re, im = 0.0, 0.0
        for which in range(ratio):
            step = (which - part if mirrored else which + part) % ratio
            re = re + got[which][2 * step * rows : (2 * step + 1) * rows]
            im = im + got[which][(2 * step + 1) * rows : (2 * step + 2) * rows]
        out_re = re[:, :lanes] - im[:, lanes:]
        out_im = re[:, lanes:] + im[:, :lanes]
        if mirrored:
            out_im = -out_im
        start = part * width
        out_ref[:, start : start + lanes] = out_re.astype(out_ref.dtype)
        out_ref[:, start + lanes : start + width] = out_im.astype(out_ref.dtype)


def windowed(spectra, table, place, rows, dtype, mirrored):
    ratio, win, width = table.shape
    length = ratio * win
    return pl.pallas_call(
        functools.partial(window_kernel, mirrored),
        out_shape=jax.ShapeDtypeStruct((rows, ratio * width), dtype),
        grid_spec=pltpu.PrefetchScalarGridSpec(
            num_scalar_prefetch=1,
            grid=(1,),
            in_specs=[
                pl.BlockSpec((1, 2, rows, length), lambda a, place: (place[0], 0, place[1], 0)),
                pl.BlockSpec(table.shape, lambda a, place: (0, 0, 0)),
            ],
            out_specs=pl.BlockSpec((rows, ratio * width), lambda a, place: (0, 0)),
        ),
        compiler_params=params(WINDOW_MB),
        cost_estimate=pl.CostEstimate(
            flops=4 * rows * length * ratio * width,
            bytes_accessed=2 * (2 * rows * length + length * width),
            transcendentals=0,
        ),
        name="windowed",
    )(place, spectra, table)


def template_kernel(index_ref, bank_ref, left_ref, right_ref, low_ref, high_ref, hold_low, hold_high):
    ratio, depth, width = right_ref.shape
    window, low = hold_low.shape[0], hold_low.shape[1]
    rows = left_ref.shape[1]
    left = jnp.concatenate([left_ref[0], left_ref[1]], 0)
    for o in range(window):
        values = bank_ref[index_ref[o]].astype(jnp.float32)
        centred = values - jnp.mean(values)
        factor = lax.rsqrt(jnp.mean(centred * centred) + 1e-06)
        template = (centred * factor).astype(jnp.bfloat16)
        rowpass = jnp.dot(left, template, preferred_element_type=jnp.float32).astype(jnp.bfloat16)
        both = jnp.concatenate([rowpass[:rows], rowpass[rows:]], 1)
        hold_low[o] = both[:low]
        hold_high[o] = both[low:]
    for hold, out in ((hold_low, low_ref), (hold_high, high_ref)):
        flat = hold[...].reshape(window * hold.shape[1], depth)
        for part in range(ratio):
            got = jnp.dot(flat, right_ref[part], preferred_element_type=jnp.float32)
            out[part] = got.astype(out.dtype)


def template_spectra(bank, orient_index, left, band, win, lanes, dtype):
    tsize = bank.shape[1]
    window = orient_index.shape[0]
    ratio = win // lanes
    right = template_table(tsize, win, lanes).reshape(2 * tsize, ratio, 2 * lanes)
    right = jnp.asarray(np.ascontiguousarray(right.transpose(1, 0, 2)))
    low, high = band // 2, band // 2 + PAD
    return pl.pallas_call(
        template_kernel,
        out_shape=[
            jax.ShapeDtypeStruct((ratio, window * low, 2 * lanes), dtype),
            jax.ShapeDtypeStruct((ratio, window * high, 2 * lanes), dtype),
        ],
        in_specs=[SMEM] + vmem(3),
        out_specs=vmem(2),
        scratch_shapes=[
            pltpu.VMEM((window, low, 2 * tsize), jnp.bfloat16),
            pltpu.VMEM((window, high, 2 * tsize), jnp.bfloat16),
        ],
        compiler_params=params(TEMPLATE_MB),
        cost_estimate=pl.CostEstimate(
            flops=2 * window * (band + PAD) * tsize * (2 * tsize + 4 * win),
            bytes_accessed=2 * (bank.size + window * (band + PAD) * 2 * win),
            transcendentals=0,
        ),
        name="templates",
    )(orient_index, bank, left, right)


def partial_kernel(count, first, keep_ref, flip_ref, tspec_ref, back_ref, *rest):
    other_refs, rest = rest[:count], rest[count:]
    part_ref, outs = rest[-1], rest[:-1]
    _, _, members, mine, _ = place()
    window = part_ref.shape[0]
    band = keep_ref.shape[0] // 2
    rows = flip_ref.shape[0]
    ratio, _, width = tspec_ref.shape
    lanes = width // 2
    received = jnp.concatenate([other[...] for other in other_refs], 0)
    held = jnp.dot(flip_ref[...], received, preferred_element_type=jnp.float32)
    head = held[:band] + keep_ref[first : first + band]
    held = head if rows == band else jnp.concatenate([head, held[band:]], 0)
    total = None
    for part in range(ratio):
        mic_re = held[:, part * width : part * width + lanes]
        mic_im = held[:, part * width + lanes : (part + 1) * width]
        upper, lower = [], []
        for o in range(window):
            tmpl_re = tspec_ref[part, o * rows : (o + 1) * rows, :lanes].astype(jnp.float32)
            tmpl_im = tspec_ref[part, o * rows : (o + 1) * rows, lanes:].astype(jnp.float32)
            prod_re = mic_re * tmpl_re + mic_im * tmpl_im
            prod_im = mic_im * tmpl_re - mic_re * tmpl_im
            product = jnp.concatenate([prod_re, prod_im], 1)
            rounded = product.astype(jnp.bfloat16)
            upper.append(rounded)
            lower.append((product - rounded.astype(jnp.float32)).astype(jnp.bfloat16))
        upper = jnp.concatenate(upper, 0)
        lower = jnp.concatenate(lower, 0)
        got = jnp.dot(upper, back_ref[0, part], preferred_element_type=jnp.float32)
        got += jnp.dot(lower, back_ref[0, part], preferred_element_type=jnp.float32)
        got += jnp.dot(upper, back_ref[1, part], preferred_element_type=jnp.float32)
        total = got if total is None else total + got
    for o in range(window):
        part_ref[o] = total[o * rows : (o + 1) * rows]

    group = WCOLS // members
    lane_group = lax.broadcasted_iota(jnp.int32, (rows, WCOLS), 1) // group
    tiles = max(1, window // members)
    for tile in range(tiles):
        for plane in range(2):
            at = slice(plane * WCOLS, (plane + 1) * WCOLS)
            pieces = []
            for i in range(members):
                piece = part_ref[(tile * members + i) % window, :, at]
                pieces.append(pltpu.roll(piece, group * i, 1) if i else piece)
            for s in range(members):
                target = lax.bitwise_xor(mine, s)
                packed = pieces[0]
                for i in range(1, members):
                    inside = (lane_group + (members - i)) % members == target
                    packed = jnp.where(inside, pieces[i], packed)
                start = (plane * tiles + tile) * WCOLS
                outs[s][:, start : start + WCOLS] = packed.astype(outs[s].dtype)


def partials(keep, others, first, flip, tspec, back, members, window):
    rows = flip.shape[0]
    ratio, _, width = tspec.shape
    tiles = max(1, window // members)
    out_shape = (rows, 2 * tiles * WCOLS)
    return pl.pallas_call(
        functools.partial(partial_kernel, len(others), first),
        out_shape=[jax.ShapeDtypeStruct(out_shape, jnp.bfloat16)] * members,
        in_specs=vmem(4 + len(others)),
        out_specs=vmem(members),
        scratch_shapes=[
            pltpu.VMEM((window, rows, 2 * WCOLS), jnp.float32),
        ],
        compiler_params=params(PARTIAL_MB),
        cost_estimate=pl.CostEstimate(
            flops=12 * tspec.size * WCOLS,
            bytes_accessed=2 * tspec.size,
            transcendentals=0,
        ),
        name="partials",
    )(keep, flip, tspec, back, *others)


def column_kernel(group_of, scale, share, roots_ref, *rest):
    row, core, members, mine, side = place()
    cores, classes = lax.axis_size("orient"), lax.axis_size("row")
    many = len(group_of)
    tables, rest = rest[:many], rest[many:]
    low_parts, high_parts = rest[:members], rest[members : 2 * members]
    outs = rest[2 * members : 2 * members + many]
    held_ref, last_ref = rest[2 * members + many :]
    steps = tables[0].shape[0]
    low, width = low_parts[0].shape
    band = held_ref.shape[1]
    wide = width // 2
    for s in range(members):
        member = lax.bitwise_xor(mine, s)
        held_ref[member, :low] = low_parts[s][...]
        held_ref[member, low:] = high_parts[s][: band - low]
        last_ref[member] = high_parts[s][band - low :]
    planes = []
    for member in range(members):
        block = held_ref[member]
        if member:
            head = block[:PAD].astype(jnp.float32) + last_ref[member - 1].astype(jnp.float32)
            block = jnp.concatenate([head.astype(jnp.bfloat16), block[PAD:]], 0)
        planes.append((block[:, :wide], block[:, wide:]))
    top = last_ref[members - 1][:1, :wide].astype(jnp.float32)
    group = WCOLS // members
    height = steps // (members // 2)
    lane_group = lax.broadcasted_iota(jnp.int32, (height, WCOLS), 1) // group
    kappa = (lane_group + (members - mine)) % members
    for which in range(many):
        rho = reverse_bits(lax.bitwise_xor(row, group_of[which]), bits(classes))
        corr = (1 - 2 * (rho % 2)).astype(jnp.float32) * top
        for turn in range(members // cores):
            angle = rho * turn % classes
            cos = roots_ref[0, angle].astype(jnp.bfloat16)
            sin = roots_ref[1, angle].astype(jnp.bfloat16)
            blocks = []
            for re, im in planes[turn * cores : (turn + 1) * cores]:
                blocks += [cos * re - sin * im, sin * re + cos * im] if turn else [re, im]
            stacked = jnp.concatenate(blocks, 0)
            corr = corr + jnp.dot(tables[which][...], stacked, preferred_element_type=jnp.float32)
        corr = corr * (scale * (1 - 2 * (side * rho % 2)).astype(jnp.float32))
        peak = corr[:, :WCOLS]
        power = corr[:, :WCOLS] * corr[:, :WCOLS]
        for start in range(WCOLS, wide, WCOLS):
            more = corr[:, start : start + WCOLS]
            peak = jnp.maximum(peak, more)
            power = power + more * more
        shift = group
        while shift < WCOLS:
            peak = jnp.maximum(peak, pltpu.roll(peak, shift, 1))
            power = power + pltpu.roll(power, shift, 1)
            shift *= 2
        if share != 1.0:
            power = power * share
        packed = peak[:height]
        for k in range(1, members):
            source = (power if k % 2 else peak)[k // 2 * height : (k // 2 + 1) * height]
            packed = jnp.where(kappa == k, source, packed)
        outs[which][...] = packed.astype(outs[which].dtype)


def columns(parts, tables, group_of, classes, band, scale, share, dtype):
    members = len(parts) // 2
    many = len(group_of)
    steps = tables[0].shape[0]
    height = steps // (members // 2)
    width = parts[0].shape[1]
    roots = np.round(np.exp(2j * np.pi * np.arange(classes) / classes), 12)
    roots = jnp.asarray(np.stack([roots.real, roots.imag]).astype(np.float32))
    return pl.pallas_call(
        functools.partial(column_kernel, group_of, scale, share),
        out_shape=[jax.ShapeDtypeStruct((height, WCOLS), dtype)] * many,
        in_specs=[SMEM] + vmem(many + 2 * members),
        out_specs=vmem(many),
        scratch_shapes=[
            pltpu.VMEM((members, band, width), jnp.bfloat16),
            pltpu.VMEM((members, PAD, width), jnp.bfloat16),
        ],
        compiler_params=params(COLUMN_MB),
        cost_estimate=pl.CostEstimate(
            flops=many * 2 * tables[0].size * width // 2,
            bytes_accessed=2 * many * tables[0].size,
            transcendentals=0,
        ),
        name="columns",
    )(roots, *tables, *parts)


def unpack_kernel(classes, *rest):
    near = rest[:classes]
    far = rest[classes : 2 * classes]
    peak_ref, power_ref = rest[2 * classes :]
    row, core, members, _, side = place()
    half = classes // 2
    height = near[0].shape[0]
    group = WCOLS // members
    lane_group = lax.broadcasted_iota(jnp.int32, (height, WCOLS), 1) // group
    for delta in range(2):
        mic = lax.bitwise_xor(side, delta)
        for k in range(members):
            wanted = (lane_group + (members - k)) % members
            value = jnp.zeros((height, WCOLS), jnp.float32)
            for low in range(half):
                s = delta * half + low
                base = lax.bitwise_xor(row, s) % half * 2
                for source, at in ((near, core), (far, 1 - core)):
                    value = jnp.where(wanted == base + at, source[s][...].astype(jnp.float32), value)
            if k:
                value = pltpu.roll(value, WCOLS - k * group, 1)
            target = power_ref if k % 2 else peak_ref
            target[mic, 0, k // 2 * height : (k // 2 + 1) * height, :] = value


def unpack(near, far, steps):
    classes = len(near)
    shape = jax.ShapeDtypeStruct((2, 1, steps, WCOLS), jnp.float32)
    return pl.pallas_call(
        functools.partial(unpack_kernel, classes),
        out_shape=[shape, shape],
        in_specs=vmem(2 * classes),
        out_specs=vmem(2),
        compiler_params=params(8),
        name="unpack",
    )(*near, *far)


def shards(spectra, bank, orient_index):
    length = spectra.shape[3]
    tsize = bank.shape[1]
    classes = lax.axis_size("row")
    cores = lax.axis_size("orient")
    count = classes * cores
    members = count // 2
    band = length // count
    steps = length // classes
    win = 1 << (tsize + WCOLS - 2).bit_length()
    lanes = win // (length // win)
    line = ("row", "orient")
    window = orient_index.shape[0]
    rows = band // 2

    row, core, _, _, side = place()
    device = row * cores + core
    mirror_table = jnp.asarray(window_table(length, win, True))
    table = jnp.asarray(window_table(length, win, False))
    back = jnp.asarray(back_table(win, lanes))
    flip = flip_table(band)

    opposite = [(i, count - 1 - i) for i in range(count)]
    others = []
    for block in (1, 0):
        at = jnp.stack([1 - side, 2 * core + block]).astype(jnp.int32)
        sent = windowed(spectra, mirror_table, at, rows, jnp.bfloat16, True)
        others.insert(0, lax.ppermute(sent, line, opposite))
    cos, sin = phases(np.arange(length + PAD), np.arange(tsize), length)
    left = jnp.asarray(np.stack([cos, -sin]).astype(BF16))
    left = lax.dynamic_slice_in_dim(left, device * band, band + PAD, 1)
    spectra, bank, left, _ = lax.optimization_barrier((spectra, bank, left, sent))
    at = jnp.stack([side, core]).astype(jnp.int32)
    keep = windowed(spectra, table, at, band, jnp.float32, False)
    bank, left, keep = lax.optimization_barrier((bank, left, keep))
    tspec = template_spectra(bank, orient_index, left, band, win, lanes, jnp.float32)
    lows, highs = [], []
    for block, got in ((0, lows), (1, highs)):
        parts = partials(
            keep,
            others[1 - block :],
            block * rows,
            jnp.asarray(flip[:rows, rows:] if block == 0 else flip[rows:]),
            tspec[block],
            back,
            members,
            window,
        )
        got.append(parts[0])
        for s in range(1, members):
            got.append(lax.ppermute(parts[s], line, [(i, i ^ s) for i in range(count)]))

    all_tables = jnp.asarray(column_table(length, classes, cores, band))
    row, _ = lax.optimization_barrier((row, parts[0]))
    maps = [None] * classes
    for group in (range(classes // 2, classes), range(classes // 2)):
        rhos = [reverse_bits(lax.bitwise_xor(row, s), bits(classes)) for s in group]
        made = columns(
            lows + highs,
            [lax.dynamic_index_in_dim(all_tables, rho, 0, False) for rho in rhos],
            tuple(group),
            classes,
            band,
            1.0 / (length * tsize),
            window / max(window, members),
            jnp.float32,
        )
        for s, one in zip(group, made):
            maps[s] = one
    near = [maps[0]]
    for s in range(1, classes):
        near.append(lax.ppermute(maps[s], "row", [(i, i ^ s) for i in range(classes)]))
    far = [lax.ppermute(m, "orient", [(0, 1), (1, 0)]) for m in near]
    peak, power = unpack(near, far, steps)
    return peak, power


def solution(mesh):
    return jax.shard_map(
        shards,
        mesh=mesh,
        in_specs=(P(("grp", "mic"), None, "row", None), P(), P("grp")),
        out_specs=(P(("grp", "mic"), "row", None, None), P(("grp", "mic"), "row", None, None)),
        check_vma=False,
    )
```

```python
import functools
import math

import jax
import jax.numpy as jnp
import ml_dtypes
import numpy as np
from jax import lax
from jax.experimental import pallas as pl
from jax.experimental.pallas import tpu as pltpu
from jax.sharding import PartitionSpec as P

WCOLS = 128
WINDOW_MB = 57
TEMPLATE_MB = 16
PARTIAL_MB = 16
COLUMN_MB = 12
PAD = 16

two_pi = 2.0 * math.pi
BF16 = ml_dtypes.bfloat16


def params(mebibytes):
    return pltpu.CompilerParams(vmem_limit_bytes=mebibytes * 1024 * 1024)


def bits(count):
    return count.bit_length() - 1


def reverse_bits(number, digits):
    result = number * 0
    for digit in range(digits):
        result = result + number // (1 << digit) % 2 * (1 << digits - 1 - digit)
    return result


def phases(rows, cols, period):
    angles = np.outer(rows, cols) % period * (two_pi / period)
    return np.cos(angles), np.sin(angles)


def window_table(length, win, mirrored):
    ratio = length // win
    lanes = win // ratio
    sign = 1 if mirrored else -1
    base = np.arange(win)[:, None] + sign * ratio * np.arange(lanes)[None, :]
    d = (length // ratio * np.arange(ratio)[:, None, None] + base[None]) % length
    u = np.arange(win)
    kernel = np.exp(2j * np.pi * (np.outer(np.arange(length), u) % length) / length).sum(1) / win
    val = kernel[d]
    return np.concatenate([val.real, val.imag], 2).astype(BF16)


def tiles_of(re, im, lanes, axis):
    pieces = []
    for start in range(0, re.shape[axis], lanes):
        cut = [slice(None)] * re.ndim
        cut[axis] = slice(start, start + lanes)
        pieces += [re[tuple(cut)], im[tuple(cut)]]
    return np.concatenate(pieces, axis)


def template_table(tsize, win, lanes):
    cos, sin = phases(np.arange(tsize), np.arange(win), win)
    upper = tiles_of(cos, -sin, lanes, 1)
    lower = tiles_of(sin, cos, lanes, 1)
    return np.concatenate([upper, lower], 0).astype(BF16)


def split(table):
    upper = table.astype(BF16)
    return np.stack([upper, (table - upper.astype(np.float64)).astype(BF16)])


def back_table(win, lanes):
    cos, sin = phases(np.arange(win), np.arange(WCOLS), win)
    re_rows = np.concatenate([cos, sin], 1)
    im_rows = np.concatenate([-sin, cos], 1)
    table = tiles_of(re_rows, im_rows, lanes, 0)
    return split(table.reshape(win // lanes, 2 * lanes, 2 * WCOLS))


def column_table(length, classes, cores, band):
    steps = length // classes
    freqs = np.arange(cores * band)
    out = []
    for rho in range(classes):
        cos, sin = phases(rho + classes * np.arange(steps), freqs, length)
        out.append(tiles_of(cos, -sin, band, 1))
    return np.stack(out).astype(BF16)


def flip_table(band):
    out = np.zeros((band + PAD, band), np.float32)
    out[band - np.arange(band), np.arange(band)] = 1.0
    return out.astype(BF16)


def vmem(count):
    return [pl.BlockSpec(memory_space=pltpu.VMEM)] * count


def hbm(count):
    return [pl.BlockSpec(memory_space=pltpu.HBM)] * count


SMEM = pl.BlockSpec(memory_space=pltpu.SMEM)


def place():
    row, core = lax.axis_index("row"), lax.axis_index("orient")
    cores = lax.axis_size("orient")
    members = lax.axis_size("row") * cores // 2
    device = row * cores + core
    return row, core, members, device % members, device // members


def window_block(mirrored, spec, table, out_ref):
    rows, total = out_ref.shape
    ratio = table(None)
    width = total // ratio
    lanes = width // 2
    win = ratio * lanes
    pieces = []
    for step in range(ratio):
        at = slice(step * win, (step + 1) * win)
        pieces += [spec(part, at) for part in range(2)]
    stacked = jnp.concatenate(pieces, 0)
    got = [
        jnp.dot(stacked, table(which), preferred_element_type=jnp.float32)
        for which in range(ratio)
    ]
    for part in range(ratio):
        re, im = 0.0, 0.0
        for which in range(ratio):
            step = (which - part if mirrored else which + part) % ratio
            re = re + got[which][2 * step * rows : (2 * step + 1) * rows]
            im = im + got[which][(2 * step + 1) * rows : (2 * step + 2) * rows]
        out_re = re[:, :lanes] - im[:, lanes:]
        out_im = re[:, lanes:] + im[:, :lanes]
        if mirrored:
            out_im = -out_im
        start = part * width
        out_ref[:, start : start + lanes] = out_re.astype(out_ref.dtype)
        out_ref[:, start + lanes : start + width] = out_im.astype(out_ref.dtype)


def first_kernel(spec_ref, tables_ref, out_ref, held_ref, table_ref, sem):
    rows = out_ref.shape[0]
    _, core, _, _, side = place()
    start = pl.multiple_of((2 * core + 1) * rows, rows)
    copies = [
        pltpu.make_async_copy(
            spec_ref.at[1 - side, :, pl.ds(start, rows)], held_ref, sem.at[0]
        ),
        pltpu.make_async_copy(tables_ref.at[0], table_ref, sem.at[1]),
    ]
    for copy in copies:
        copy.start()
    for copy in copies:
        copy.wait()
    window_block(
        True,
        lambda part, at: held_ref[part, :, at],
        lambda k: table_ref.shape[0] if k is None else table_ref[k],
        out_ref,
    )


def window_first(spectra, tables, rows):
    _, ratio, win, width = tables.shape
    return pl.pallas_call(
        first_kernel,
        out_shape=jax.ShapeDtypeStruct((rows, ratio * width), jnp.bfloat16),
        in_specs=hbm(2),
        out_specs=vmem(1)[0],
        scratch_shapes=[
            pltpu.VMEM((2, rows, ratio * win), jnp.bfloat16),
            pltpu.VMEM((ratio, win, width), jnp.bfloat16),
            pltpu.SemaphoreType.DMA((2,)),
        ],
        compiler_params=params(WINDOW_MB),
        cost_estimate=pl.CostEstimate(
            flops=4 * rows * ratio * win * ratio * width,
            bytes_accessed=8 * rows * ratio * win,
            transcendentals=0,
        ),
        name="window_first",
    )(spectra, tables)


def rest_kernel(place_ref, spec_ref, table_ref, main_ref, more_ref, *outs):
    sent_ref, keep_ref, low_ref, high_ref = outs
    step = pl.program_id(0)
    spec = lambda part, at: spec_ref[0, part, :, at]
    table = lambda k: table_ref.shape[1] if k is None else table_ref[0, k]

    @pl.when(step == 0)
    def _():
        window_block(True, spec, table, sent_ref)
        low, band = low_ref.shape[1], main_ref.shape[1]
        low_ref[...] = main_ref[:, :low]
        high_ref[:, : band - low] = main_ref[:, low:]
        high_ref[:, band - low :] = more_ref[...]

    @pl.when(step > 0)
    def _():
        window_block(False, spec, table, keep_ref)


def window_rest(spectra, tables, left, rows):
    _, ratio, win, width = tables.shape
    row, core, members, _, side = place()
    device = row * lax.axis_size("orient") + core
    band = 2 * rows
    tsize = left.shape[2]
    at = jnp.stack([side, core, device]).astype(jnp.int32)

    def spec_index(i, at):
        first = jnp.where(i == 0, 1, 0)
        return at[0] + first * (1 - 2 * at[0]), 0, 2 * at[1] + jnp.maximum(i - 1, 0), 0

    return pl.pallas_call(
        rest_kernel,
        out_shape=[
            jax.ShapeDtypeStruct((rows, ratio * width), jnp.bfloat16),
            jax.ShapeDtypeStruct((band, ratio * width), jnp.float32),
            jax.ShapeDtypeStruct((2, rows, tsize), jnp.bfloat16),
            jax.ShapeDtypeStruct((2, rows + PAD, tsize), jnp.bfloat16),
        ],
        grid_spec=pltpu.PrefetchScalarGridSpec(
            num_scalar_prefetch=1,
            grid=(3,),
            in_specs=[
                pl.BlockSpec((1, 2, rows, ratio * win), spec_index),
                pl.BlockSpec((1, ratio, win, width), lambda i, at: (jnp.minimum(i, 1), 0, 0, 0)),
                pl.BlockSpec((2, band, tsize), lambda i, at: (0, at[2], 0)),
                pl.BlockSpec((2, PAD, tsize), lambda i, at: (0, (at[2] + 1) * (band // PAD), 0)),
            ],
            out_specs=[
                pl.BlockSpec((rows, ratio * width), lambda i, at: (0, 0)),
                pl.BlockSpec((rows, ratio * width), lambda i, at: (jnp.maximum(i - 1, 0), 0)),
                pl.BlockSpec((2, rows, tsize), lambda i, at: (0, 0, 0)),
                pl.BlockSpec((2, rows + PAD, tsize), lambda i, at: (0, 0, 0)),
            ],
        ),
        compiler_params=params(WINDOW_MB),
        cost_estimate=pl.CostEstimate(
            flops=12 * rows * ratio * win * ratio * width,
            bytes_accessed=20 * rows * ratio * win,
            transcendentals=0,
        ),
        name="window_rest",
    )(at, spectra, tables, left, left)


def template_kernel(fresh, index_ref, bank_ref, left_ref, right_ref, out_ref, *rest):
    hold_ref = rest[-1]
    ratio, depth, width = right_ref.shape
    window, rows = hold_ref.shape[0], hold_ref.shape[1]
    left = jnp.concatenate([left_ref[0], left_ref[1]], 0)
    for o in range(window):
        if fresh:
            values = bank_ref[index_ref[o]].astype(jnp.float32)
            share = 1.0 / values.size
            total = jnp.sum(jnp.sum(values, 0, keepdims=True), 1, keepdims=True)
            centred = values - total * share
            square = jnp.sum(jnp.sum(centred * centred, 0, keepdims=True), 1, keepdims=True)
            factor = lax.rsqrt(square * share + 1e-06)
            template = (centred * factor).astype(jnp.bfloat16)
            rest[0][o] = template
        else:
            template = bank_ref[o]
        rowpass = jnp.dot(left, template, preferred_element_type=jnp.float32).astype(jnp.bfloat16)
        hold_ref[o] = jnp.concatenate([rowpass[:rows], rowpass[rows:]], 1)
    flat = hold_ref[...].reshape(window * rows, depth)
    for part in range(ratio):
        got = jnp.dot(flat, right_ref[part], preferred_element_type=jnp.float32)
        out_ref[part] = got.astype(out_ref.dtype)


def template_spectra(bank, orient_index, left, win, lanes, dtype, fresh):
    tsize = bank.shape[1]
    window = orient_index.shape[0]
    ratio = win // lanes
    rows = left.shape[1]
    right = template_table(tsize, win, lanes).reshape(2 * tsize, ratio, 2 * lanes)
    right = jnp.asarray(np.ascontiguousarray(right.transpose(1, 0, 2)))
    out_shape = [jax.ShapeDtypeStruct((ratio, window * rows, 2 * lanes), dtype)]
    if fresh:
        out_shape.append(jax.ShapeDtypeStruct((window, tsize, tsize), jnp.bfloat16))
    return pl.pallas_call(
        functools.partial(template_kernel, fresh),
        out_shape=out_shape,
        in_specs=[SMEM] + vmem(3),
        out_specs=vmem(len(out_shape)),
        scratch_shapes=[pltpu.VMEM((window, rows, 2 * tsize), jnp.bfloat16)],
        compiler_params=params(TEMPLATE_MB),
        cost_estimate=pl.CostEstimate(
            flops=2 * window * rows * tsize * (2 * tsize + 4 * win),
            bytes_accessed=2 * bank.size + 4 * window * rows * 2 * win,
            transcendentals=0,
        ),
        name="templates",
    )(orient_index, bank, left, right)


def partial_kernel(count, first, keep_ref, flip_ref, tspec_ref, back_ref, *rest):
    other_refs, rest = rest[:count], rest[count:]
    part_ref, outs = rest[-1], rest[:-1]
    _, _, members, mine, _ = place()
    window = part_ref.shape[0]
    band = keep_ref.shape[0] // 2
    rows = flip_ref.shape[0]
    ratio, _, width = tspec_ref.shape
    lanes = width // 2
    received = jnp.concatenate([other[...] for other in other_refs], 0)
    held = jnp.dot(flip_ref[...], received, preferred_element_type=jnp.float32)
    head = held[:band] + keep_ref[first : first + band]
    held = head if rows == band else jnp.concatenate([head, held[band:]], 0)
    total = None
    for part in range(ratio):
        mic_re = held[:, part * width : part * width + lanes]
        mic_im = held[:, part * width + lanes : (part + 1) * width]
        upper, lower = [], []
        for o in range(window):
            tmpl_re = tspec_ref[part, o * rows : (o + 1) * rows, :lanes].astype(jnp.float32)
            tmpl_im = tspec_ref[part, o * rows : (o + 1) * rows, lanes:].astype(jnp.float32)
            prod_re = mic_re * tmpl_re + mic_im * tmpl_im
            prod_im = mic_im * tmpl_re - mic_re * tmpl_im
            product = jnp.concatenate([prod_re, prod_im], 1)
            rounded = product.astype(jnp.bfloat16)
            upper.append(rounded)
            lower.append((product - rounded.astype(jnp.float32)).astype(jnp.bfloat16))
        upper = jnp.concatenate(upper, 0)
        lower = jnp.concatenate(lower, 0)
        got = jnp.dot(upper, back_ref[0, part], preferred_element_type=jnp.float32)
        got += jnp.dot(lower, back_ref[0, part], preferred_element_type=jnp.float32)
        got += jnp.dot(upper, back_ref[1, part], preferred_element_type=jnp.float32)
        total = got if total is None else total + got
    for o in range(window):
        part_ref[o] = total[o * rows : (o + 1) * rows]

    group = WCOLS // members
    lane_group = lax.broadcasted_iota(jnp.int32, (rows, WCOLS), 1) // group
    tiles = max(1, window // members)
    for tile in range(tiles):
        for plane in range(2):
            at = slice(plane * WCOLS, (plane + 1) * WCOLS)
            pieces = []
            for i in range(members):
                piece = part_ref[(tile * members + i) % window, :, at]
                pieces.append(pltpu.roll(piece, group * i, 1) if i else piece)
            for s in range(members):
                target = lax.bitwise_xor(mine, s)
                packed = pieces[0]
                for i in range(1, members):
                    inside = (lane_group + (members - i)) % members == target
                    packed = jnp.where(inside, pieces[i], packed)
                start = (plane * tiles + tile) * WCOLS
                outs[s][:, start : start + WCOLS] = packed.astype(outs[s].dtype)


def partials(keep, others, first, flip, tspec, back, members, window):
    rows = flip.shape[0]
    ratio, _, width = tspec.shape
    tiles = max(1, window // members)
    out_shape = (rows, 2 * tiles * WCOLS)
    return pl.pallas_call(
        functools.partial(partial_kernel, len(others), first),
        out_shape=[jax.ShapeDtypeStruct(out_shape, jnp.bfloat16)] * members,
        in_specs=vmem(4 + len(others)),
        out_specs=vmem(members),
        scratch_shapes=[
            pltpu.VMEM((window, rows, 2 * WCOLS), jnp.float32),
        ],
        compiler_params=params(PARTIAL_MB),
        cost_estimate=pl.CostEstimate(
            flops=12 * tspec.size * WCOLS,
            bytes_accessed=2 * tspec.size,
            transcendentals=0,
        ),
        name="partials",
    )(keep, flip, tspec, back, *others)


def column_kernel(group_of, scale, share, roots_ref, *rest):
    row, core, members, mine, side = place()
    cores, classes = lax.axis_size("orient"), lax.axis_size("row")
    many = len(group_of)
    tables, rest = rest[:many], rest[many:]
    low_parts, high_parts = rest[:members], rest[members : 2 * members]
    outs = rest[2 * members : 2 * members + many]
    held_ref, last_ref = rest[2 * members + many :]
    steps = tables[0].shape[0]
    low, width = low_parts[0].shape
    band = held_ref.shape[1]
    wide = width // 2
    for s in range(members):
        member = lax.bitwise_xor(mine, s)
        held_ref[member, :low] = low_parts[s][...]
        held_ref[member, low:] = high_parts[s][: band - low]
        last_ref[member] = high_parts[s][band - low :]
    planes = []
    for member in range(members):
        block = held_ref[member]
        if member:
            head = block[:PAD].astype(jnp.float32) + last_ref[member - 1].astype(jnp.float32)
            block = jnp.concatenate([head.astype(jnp.bfloat16), block[PAD:]], 0)
        planes.append((block[:, :wide], block[:, wide:]))
    top = last_ref[members - 1][:1, :wide].astype(jnp.float32)
    group = WCOLS // members
    height = steps // (members // 2)
    lane_group = lax.broadcasted_iota(jnp.int32, (height, WCOLS), 1) // group
    kappa = (lane_group + (members - mine)) % members
    for which in range(many):
        rho = reverse_bits(lax.bitwise_xor(row, group_of[which]), bits(classes))
        corr = (1 - 2 * (rho % 2)).astype(jnp.float32) * top
        for turn in range(members // cores):
            angle = rho * turn % classes
            cos = roots_ref[0, angle].astype(jnp.bfloat16)
            sin = roots_ref[1, angle].astype(jnp.bfloat16)
            blocks = []
            for re, im in planes[turn * cores : (turn + 1) * cores]:
                blocks += [cos * re - sin * im, sin * re + cos * im] if turn else [re, im]
            stacked = jnp.concatenate(blocks, 0)
            corr = corr + jnp.dot(tables[which][...], stacked, preferred_element_type=jnp.float32)
        corr = corr * (scale * (1 - 2 * (side * rho % 2)).astype(jnp.float32))
        peak = corr[:, :WCOLS]
        power = corr[:, :WCOLS] * corr[:, :WCOLS]
        for start in range(WCOLS, wide, WCOLS):
            more = corr[:, start : start + WCOLS]
            peak = jnp.maximum(peak, more)
            power = power + more * more
        shift = group
        while shift < WCOLS:
            peak = jnp.maximum(peak, pltpu.roll(peak, shift, 1))
            power = power + pltpu.roll(power, shift, 1)
            shift *= 2
        if share != 1.0:
            power = power * share
        packed = peak[:height]
        for k in range(1, members):
            source = (power if k % 2 else peak)[k // 2 * height : (k // 2 + 1) * height]
            packed = jnp.where(kappa == k, source, packed)
        outs[which][...] = packed.astype(outs[which].dtype)


def columns(parts, tables, group_of, classes, band, scale, share, dtype):
    members = len(parts) // 2
    many = len(group_of)
    steps = tables[0].shape[0]
    height = steps // (members // 2)
    width = parts[0].shape[1]
    roots = np.round(np.exp(2j * np.pi * np.arange(classes) / classes), 12)
    roots = jnp.asarray(np.stack([roots.real, roots.imag]).astype(np.float32))
    return pl.pallas_call(
        functools.partial(column_kernel, group_of, scale, share),
        out_shape=[jax.ShapeDtypeStruct((height, WCOLS), dtype)] * many,
        in_specs=[SMEM] + vmem(many + 2 * members),
        out_specs=vmem(many),
        scratch_shapes=[
            pltpu.VMEM((members, band, width), jnp.bfloat16),
            pltpu.VMEM((members, PAD, width), jnp.bfloat16),
        ],
        compiler_params=params(COLUMN_MB),
        cost_estimate=pl.CostEstimate(
            flops=many * 2 * tables[0].size * width // 2,
            bytes_accessed=2 * many * tables[0].size,
            transcendentals=0,
        ),
        name="columns",
    )(roots, *tables, *parts)


def unpack_kernel(classes, *rest):
    near = rest[:classes]
    far = rest[classes : 2 * classes]
    peak_ref, power_ref = rest[2 * classes :]
    row, core, members, _, side = place()
    half = classes // 2
    height = near[0].shape[0]
    group = WCOLS // members
    lane_group = lax.broadcasted_iota(jnp.int32, (height, WCOLS), 1) // group
    for delta in range(2):
        mic = lax.bitwise_xor(side, delta)
        for k in range(members):
            wanted = (lane_group + (members - k)) % members
            value = jnp.zeros((height, WCOLS), jnp.float32)
            for low in range(half):
                s = delta * half + low
                base = lax.bitwise_xor(row, s) % half * 2
                for source, at in ((near, core), (far, 1 - core)):
                    value = jnp.where(wanted == base + at, source[s][...].astype(jnp.float32), value)
            if k:
                value = pltpu.roll(value, WCOLS - k * group, 1)
            target = power_ref if k % 2 else peak_ref
            target[mic, 0, k // 2 * height : (k // 2 + 1) * height, :] = value


def unpack(near, far, steps):
    classes = len(near)
    shape = jax.ShapeDtypeStruct((2, 1, steps, WCOLS), jnp.float32)
    return pl.pallas_call(
        functools.partial(unpack_kernel, classes),
        out_shape=[shape, shape],
        in_specs=vmem(2 * classes),
        out_specs=vmem(2),
        compiler_params=params(8),
        name="unpack",
    )(*near, *far)


def shards(spectra, bank, orient_index):
    length = spectra.shape[3]
    tsize = bank.shape[1]
    classes = lax.axis_size("row")
    cores = lax.axis_size("orient")
    count = classes * cores
    members = count // 2
    band = length // count
    steps = length // classes
    win = 1 << (tsize + WCOLS - 2).bit_length()
    lanes = win // (length // win)
    line = ("row", "orient")
    window = orient_index.shape[0]
    rows = band // 2

    row = lax.axis_index("row")
    window_tables = jnp.asarray(
        np.stack([window_table(length, win, True), window_table(length, win, False)])
    )
    back = jnp.asarray(back_table(win, lanes))
    flip = flip_table(band)

    opposite = [(i, count - 1 - i) for i in range(count)]
    cos, sin = phases(np.arange(length + PAD), np.arange(tsize), length)
    left = jnp.asarray(np.stack([cos, -sin]).astype(BF16))
    sent = window_first(spectra, window_tables, rows)
    others = [lax.ppermute(sent, line, opposite)]
    spectra, bank, _ = lax.optimization_barrier((spectra, bank, sent))
    sent, keep, *left = window_rest(spectra, window_tables, left, rows)
    others.insert(0, lax.ppermute(sent, line, opposite))
    bank, keep, *left = lax.optimization_barrier((bank, keep, *left))
    lows, highs = [], []
    for block, got in ((0, lows), (1, highs)):
        tspec, *fresh = template_spectra(
            bank, orient_index, left[block], win, lanes, jnp.float32, block == 0
        )
        parts = partials(
            keep,
            others[1 - block :],
            block * rows,
            jnp.asarray(flip[:rows, rows:] if block == 0 else flip[rows:]),
            tspec,
            back,
            members,
            window,
        )
        got.append(parts[0])
        for s in range(1, members):
            got.append(lax.ppermute(parts[s], line, [(i, i ^ s) for i in range(count)]))
        if block == 0:
            bank, left[1], _ = lax.optimization_barrier((fresh[0], left[1], parts[0]))
            early = lows[1 : members // 2 + 1]
            others[0], *early = lax.optimization_barrier((others[0], *early))
            lows[1 : members // 2 + 1] = early

    all_tables = jnp.asarray(column_table(length, classes, cores, band))
    row, _ = lax.optimization_barrier((row, parts[0]))
    maps = [None] * classes
    for group in (range(classes // 2, classes), range(classes // 2)):
        rhos = [reverse_bits(lax.bitwise_xor(row, s), bits(classes)) for s in group]
        made = columns(
            lows + highs,
            [lax.dynamic_index_in_dim(all_tables, rho, 0, False) for rho in rhos],
            tuple(group),
            classes,
            band,
            1.0 / (length * tsize),
            window / max(window, members),
            jnp.float32,
        )
        for s, one in zip(group, made):
            maps[s] = one
    near = [maps[0]]
    for s in range(1, classes):
        near.append(lax.ppermute(maps[s], "row", [(i, i ^ s) for i in range(classes)]))
    far = [lax.ppermute(m, "orient", [(0, 1), (1, 0)]) for m in near]
    peak, power = unpack(near, far, steps)
    return peak, power


def solution(mesh):
    return jax.shard_map(
        shards,
        mesh=mesh,
        in_specs=(P(("grp", "mic"), None, "row", None), P(), P("grp")),
        out_specs=(P(("grp", "mic"), "row", None, None), P(("grp", "mic"), "row", None, None)),
        check_vma=False,
    )
```

```python
import functools
import math

import jax
import jax.numpy as jnp
import ml_dtypes
import numpy as np
from jax import lax
from jax.experimental import pallas as pl
from jax.experimental.pallas import tpu as pltpu
from jax.sharding import PartitionSpec as P

WCOLS = 128
WINDOW_MB = 57
TEMPLATE_MB = 16
PARTIAL_MB = 16
COLUMN_MB = 12
PAD = 16

two_pi = 2.0 * math.pi
BF16 = ml_dtypes.bfloat16


def params(mebibytes):
    return pltpu.CompilerParams(vmem_limit_bytes=mebibytes * 1024 * 1024)


def bits(count):
    return count.bit_length() - 1


def reverse_bits(number, digits):
    result = number * 0
    for digit in range(digits):
        result = result + number // (1 << digit) % 2 * (1 << digits - 1 - digit)
    return result


def phases(rows, cols, period):
    angles = np.outer(rows, cols) % period * (two_pi / period)
    return np.cos(angles), np.sin(angles)


def window_table(length, win, mirrored):
    ratio = length // win
    lanes = win // ratio
    sign = 1 if mirrored else -1
    base = np.arange(win)[:, None] + sign * ratio * np.arange(lanes)[None, :]
    d = (length // ratio * np.arange(ratio)[:, None, None] + base[None]) % length
    u = np.arange(win)
    kernel = np.exp(2j * np.pi * (np.outer(np.arange(length), u) % length) / length).sum(1) / win
    val = kernel[d]
    return np.concatenate([val.real, val.imag], 2).astype(BF16)


def tiles_of(re, im, lanes, axis):
    pieces = []
    for start in range(0, re.shape[axis], lanes):
        cut = [slice(None)] * re.ndim
        cut[axis] = slice(start, start + lanes)
        pieces += [re[tuple(cut)], im[tuple(cut)]]
    return np.concatenate(pieces, axis)


def template_table(tsize, win, lanes):
    cos, sin = phases(np.arange(tsize), np.arange(win), win)
    upper = tiles_of(cos, -sin, lanes, 1)
    lower = tiles_of(sin, cos, lanes, 1)
    return np.concatenate([upper, lower], 0).astype(BF16)


def split(table):
    upper = table.astype(BF16)
    return np.stack([upper, (table - upper.astype(np.float64)).astype(BF16)])


def back_table(win, lanes):
    cos, sin = phases(np.arange(win), np.arange(WCOLS), win)
    re_rows = np.concatenate([cos, sin], 1)
    im_rows = np.concatenate([-sin, cos], 1)
    table = tiles_of(re_rows, im_rows, lanes, 0)
    return split(table.reshape(win // lanes, 2 * lanes, 2 * WCOLS))


def column_table(length, classes, cores, band):
    steps = length // classes
    freqs = np.arange(cores * band)
    out = []
    for rho in range(classes):
        cos, sin = phases(rho + classes * np.arange(steps), freqs, length)
        out.append(tiles_of(cos, -sin, band, 1))
    return split(np.stack(out)).transpose(1, 0, 2, 3)


def flip_table(band):
    out = np.zeros((band + PAD, band), np.float32)
    out[band - np.arange(band), np.arange(band)] = 1.0
    return out.astype(BF16)


def vmem(count):
    return [pl.BlockSpec(memory_space=pltpu.VMEM)] * count


def hbm(count):
    return [pl.BlockSpec(memory_space=pltpu.HBM)] * count


SMEM = pl.BlockSpec(memory_space=pltpu.SMEM)


def place():
    row, core = lax.axis_index("row"), lax.axis_index("orient")
    cores = lax.axis_size("orient")
    members = lax.axis_size("row") * cores // 2
    device = row * cores + core
    return row, core, members, device % members, device // members


def window_block(mirrored, spec, table, out_ref):
    rows, total = out_ref.shape
    ratio = table(None)
    width = total // ratio
    lanes = width // 2
    win = ratio * lanes
    pieces = []
    for step in range(ratio):
        at = slice(step * win, (step + 1) * win)
        pieces += [spec(part, at) for part in range(2)]
    stacked = jnp.concatenate(pieces, 0)
    got = [
        jnp.dot(stacked, table(which), preferred_element_type=jnp.float32)
        for which in range(ratio)
    ]
    for part in range(ratio):
        re, im = 0.0, 0.0
        for which in range(ratio):
            step = (which - part if mirrored else which + part) % ratio
            re = re + got[which][2 * step * rows : (2 * step + 1) * rows]
            im = im + got[which][(2 * step + 1) * rows : (2 * step + 2) * rows]
        out_re = re[:, :lanes] - im[:, lanes:]
        out_im = re[:, lanes:] + im[:, :lanes]
        if mirrored:
            out_im = -out_im
        start = part * width
        out_ref[:, start : start + lanes] = out_re.astype(out_ref.dtype)
        out_ref[:, start + lanes : start + width] = out_im.astype(out_ref.dtype)


def first_kernel(spec_ref, tables_ref, out_ref, held_ref, table_ref, sem):
    rows = out_ref.shape[0]
    _, core, _, _, side = place()
    start = pl.multiple_of((2 * core + 1) * rows, rows)
    copies = [
        pltpu.make_async_copy(
            spec_ref.at[1 - side, :, pl.ds(start, rows)], held_ref, sem.at[0]
        ),
        pltpu.make_async_copy(tables_ref.at[0], table_ref, sem.at[1]),
    ]
    for copy in copies:
        copy.start()
    for copy in copies:
        copy.wait()
    window_block(
        True,
        lambda part, at: held_ref[part, :, at],
        lambda k: table_ref.shape[0] if k is None else table_ref[k],
        out_ref,
    )


def window_first(spectra, tables, rows):
    _, ratio, win, width = tables.shape
    return pl.pallas_call(
        first_kernel,
        out_shape=jax.ShapeDtypeStruct((rows, ratio * width), jnp.bfloat16),
        in_specs=hbm(2),
        out_specs=vmem(1)[0],
        scratch_shapes=[
            pltpu.VMEM((2, rows, ratio * win), jnp.bfloat16),
            pltpu.VMEM((ratio, win, width), jnp.bfloat16),
            pltpu.SemaphoreType.DMA((2,)),
        ],
        compiler_params=params(WINDOW_MB),
        cost_estimate=pl.CostEstimate(
            flops=4 * rows * ratio * win * ratio * width,
            bytes_accessed=8 * rows * ratio * win,
            transcendentals=0,
        ),
        name="window_first",
    )(spectra, tables)


def rest_kernel(place_ref, spec_ref, table_ref, main_ref, more_ref, *outs):
    sent_ref, keep_ref, low_ref, high_ref = outs
    step = pl.program_id(0)
    spec = lambda part, at: spec_ref[0, part, :, at]
    table = lambda k: table_ref.shape[1] if k is None else table_ref[0, k]

    @pl.when(step == 0)
    def _():
        window_block(True, spec, table, sent_ref)
        low, band = low_ref.shape[1], main_ref.shape[1]
        low_ref[...] = main_ref[:, :low]
        high_ref[:, : band - low] = main_ref[:, low:]
        high_ref[:, band - low :] = more_ref[...]

    @pl.when(step > 0)
    def _():
        window_block(False, spec, table, keep_ref)


def window_rest(spectra, tables, left, rows):
    _, ratio, win, width = tables.shape
    row, core, members, _, side = place()
    device = row * lax.axis_size("orient") + core
    band = 2 * rows
    tsize = left.shape[2]
    at = jnp.stack([side, core, device]).astype(jnp.int32)

    def spec_index(i, at):
        first = jnp.where(i == 0, 1, 0)
        return at[0] + first * (1 - 2 * at[0]), 0, 2 * at[1] + jnp.maximum(i - 1, 0), 0

    return pl.pallas_call(
        rest_kernel,
        out_shape=[
            jax.ShapeDtypeStruct((rows, ratio * width), jnp.bfloat16),
            jax.ShapeDtypeStruct((band, ratio * width), jnp.float32),
            jax.ShapeDtypeStruct((2, rows, tsize), jnp.bfloat16),
            jax.ShapeDtypeStruct((2, rows + PAD, tsize), jnp.bfloat16),
        ],
        grid_spec=pltpu.PrefetchScalarGridSpec(
            num_scalar_prefetch=1,
            grid=(3,),
            in_specs=[
                pl.BlockSpec((1, 2, rows, ratio * win), spec_index),
                pl.BlockSpec((1, ratio, win, width), lambda i, at: (jnp.minimum(i, 1), 0, 0, 0)),
                pl.BlockSpec((2, band, tsize), lambda i, at: (0, at[2], 0)),
                pl.BlockSpec((2, PAD, tsize), lambda i, at: (0, (at[2] + 1) * (band // PAD), 0)),
            ],
            out_specs=[
                pl.BlockSpec((rows, ratio * width), lambda i, at: (0, 0)),
                pl.BlockSpec((rows, ratio * width), lambda i, at: (jnp.maximum(i - 1, 0), 0)),
                pl.BlockSpec((2, rows, tsize), lambda i, at: (0, 0, 0)),
                pl.BlockSpec((2, rows + PAD, tsize), lambda i, at: (0, 0, 0)),
            ],
        ),
        compiler_params=params(WINDOW_MB),
        cost_estimate=pl.CostEstimate(
            flops=12 * rows * ratio * win * ratio * width,
            bytes_accessed=20 * rows * ratio * win,
            transcendentals=0,
        ),
        name="window_rest",
    )(at, spectra, tables, left, left)


def template_kernel(fresh, index_ref, bank_ref, left_ref, right_ref, out_ref, *rest):
    hold_ref = rest[-1]
    ratio, depth, width = right_ref.shape
    window, rows = hold_ref.shape[0], hold_ref.shape[1]
    left = jnp.concatenate([left_ref[0], left_ref[1]], 0)
    for o in range(window):
        if fresh:
            values = bank_ref[index_ref[o]].astype(jnp.float32)
            share = 1.0 / values.size
            total = jnp.sum(jnp.sum(values, 0, keepdims=True), 1, keepdims=True)
            centred = values - total * share
            square = jnp.sum(jnp.sum(centred * centred, 0, keepdims=True), 1, keepdims=True)
            factor = lax.rsqrt(square * share + 1e-06)
            template = (centred * factor).astype(jnp.bfloat16)
            rest[0][o] = template
        else:
            template = bank_ref[o]
        rowpass = jnp.dot(left, template, preferred_element_type=jnp.float32).astype(jnp.bfloat16)
        hold_ref[o] = jnp.concatenate([rowpass[:rows], rowpass[rows:]], 1)
    flat = hold_ref[...].reshape(window * rows, depth)
    for part in range(ratio):
        got = jnp.dot(flat, right_ref[part], preferred_element_type=jnp.float32)
        out_ref[part] = got.astype(out_ref.dtype)


def template_spectra(bank, orient_index, left, win, lanes, dtype, fresh):
    tsize = bank.shape[1]
    window = orient_index.shape[0]
    ratio = win // lanes
    rows = left.shape[1]
    right = template_table(tsize, win, lanes).reshape(2 * tsize, ratio, 2 * lanes)
    right = jnp.asarray(np.ascontiguousarray(right.transpose(1, 0, 2)))
    out_shape = [jax.ShapeDtypeStruct((ratio, window * rows, 2 * lanes), dtype)]
    if fresh:
        out_shape.append(jax.ShapeDtypeStruct((window, tsize, tsize), jnp.bfloat16))
    return pl.pallas_call(
        functools.partial(template_kernel, fresh),
        out_shape=out_shape,
        in_specs=[SMEM] + vmem(3),
        out_specs=vmem(len(out_shape)),
        scratch_shapes=[pltpu.VMEM((window, rows, 2 * tsize), jnp.bfloat16)],
        compiler_params=params(TEMPLATE_MB),
        cost_estimate=pl.CostEstimate(
            flops=2 * window * rows * tsize * (2 * tsize + 4 * win),
            bytes_accessed=2 * bank.size + 4 * window * rows * 2 * win,
            transcendentals=0,
        ),
        name="templates",
    )(orient_index, bank, left, right)


def partial_kernel(count, first, keep_ref, flip_ref, tspec_ref, back_ref, *rest):
    other_refs, rest = rest[:count], rest[count:]
    part_ref, outs = rest[-1], rest[:-1]
    _, _, members, mine, _ = place()
    window = part_ref.shape[0]
    band = keep_ref.shape[0] // 2
    rows = flip_ref.shape[0]
    ratio, _, width = tspec_ref.shape
    lanes = width // 2
    received = jnp.concatenate([other[...] for other in other_refs], 0)
    held = jnp.dot(flip_ref[...], received, preferred_element_type=jnp.float32)
    head = held[:band] + keep_ref[first : first + band]
    held = head if rows == band else jnp.concatenate([head, held[band:]], 0)
    total = None
    for part in range(ratio):
        mic_re = held[:, part * width : part * width + lanes]
        mic_im = held[:, part * width + lanes : (part + 1) * width]
        upper, lower = [], []
        for o in range(window):
            tmpl_re = tspec_ref[part, o * rows : (o + 1) * rows, :lanes].astype(jnp.float32)
            tmpl_im = tspec_ref[part, o * rows : (o + 1) * rows, lanes:].astype(jnp.float32)
            prod_re = mic_re * tmpl_re + mic_im * tmpl_im
            prod_im = mic_im * tmpl_re - mic_re * tmpl_im
            product = jnp.concatenate([prod_re, prod_im], 1)
            rounded = product.astype(jnp.bfloat16)
            upper.append(rounded)
            lower.append((product - rounded.astype(jnp.float32)).astype(jnp.bfloat16))
        upper = jnp.concatenate(upper, 0)
        lower = jnp.concatenate(lower, 0)
        got = jnp.dot(upper, back_ref[0, part], preferred_element_type=jnp.float32)
        got += jnp.dot(lower, back_ref[0, part], preferred_element_type=jnp.float32)
        got += jnp.dot(upper, back_ref[1, part], preferred_element_type=jnp.float32)
        total = got if total is None else total + got
    for o in range(window):
        part_ref[o] = total[o * rows : (o + 1) * rows]

    group = WCOLS // members
    lane_group = lax.broadcasted_iota(jnp.int32, (rows, WCOLS), 1) // group
    tiles = max(1, window // members)
    for tile in range(tiles):
        for plane in range(2):
            at = slice(plane * WCOLS, (plane + 1) * WCOLS)
            pieces = []
            for i in range(members):
                piece = part_ref[(tile * members + i) % window, :, at]
                pieces.append(pltpu.roll(piece, group * i, 1) if i else piece)
            for s in range(members):
                target = lax.bitwise_xor(mine, s)
                packed = pieces[0]
                for i in range(1, members):
                    inside = (lane_group + (members - i)) % members == target
                    packed = jnp.where(inside, pieces[i], packed)
                start = (plane * tiles + tile) * WCOLS
                outs[s][:, start : start + WCOLS] = packed.astype(outs[s].dtype)


def partials(keep, others, first, flip, tspec, back, members, window):
    rows = flip.shape[0]
    ratio, _, width = tspec.shape
    tiles = max(1, window // members)
    out_shape = (rows, 2 * tiles * WCOLS)
    return pl.pallas_call(
        functools.partial(partial_kernel, len(others), first),
        out_shape=[jax.ShapeDtypeStruct(out_shape, jnp.bfloat16)] * members,
        in_specs=vmem(4 + len(others)),
        out_specs=vmem(members),
        scratch_shapes=[
            pltpu.VMEM((window, rows, 2 * WCOLS), jnp.float32),
        ],
        compiler_params=params(PARTIAL_MB),
        cost_estimate=pl.CostEstimate(
            flops=12 * tspec.size * WCOLS,
            bytes_accessed=2 * tspec.size,
            transcendentals=0,
        ),
        name="partials",
    )(keep, flip, tspec, back, *others)


def column_kernel(group_of, scale, share, roots_ref, *rest):
    row, core, members, mine, side = place()
    cores, classes = lax.axis_size("orient"), lax.axis_size("row")
    many = len(group_of)
    tables, rest = rest[:many], rest[many:]
    low_parts, high_parts = rest[:members], rest[members : 2 * members]
    outs = rest[2 * members : 2 * members + many]
    held_ref, last_ref = rest[2 * members + many :]
    steps = tables[0].shape[1]
    low, width = low_parts[0].shape
    band = held_ref.shape[1]
    wide = width // 2
    for s in range(members):
        member = lax.bitwise_xor(mine, s)
        held_ref[member, :low] = low_parts[s][...]
        held_ref[member, low:] = high_parts[s][: band - low]
        last_ref[member] = high_parts[s][band - low :]
    planes = []
    for member in range(members):
        block = held_ref[member]
        if member:
            head = block[:PAD].astype(jnp.float32) + last_ref[member - 1].astype(jnp.float32)
            block = jnp.concatenate([head.astype(jnp.bfloat16), block[PAD:]], 0)
        planes.append((block[:, :wide], block[:, wide:]))
    top = last_ref[members - 1][:1, :wide].astype(jnp.float32)
    group = WCOLS // members
    height = steps // (members // 2)
    lane_group = lax.broadcasted_iota(jnp.int32, (height, WCOLS), 1) // group
    kappa = (lane_group + (members - mine)) % members
    for which in range(many):
        rho = reverse_bits(lax.bitwise_xor(row, group_of[which]), bits(classes))
        corr = (1 - 2 * (rho % 2)).astype(jnp.float32) * top
        for turn in range(members // cores):
            angle = rho * turn % classes
            cos = roots_ref[0, angle].astype(jnp.bfloat16)
            sin = roots_ref[1, angle].astype(jnp.bfloat16)
            blocks = []
            for re, im in planes[turn * cores : (turn + 1) * cores]:
                blocks += [cos * re - sin * im, sin * re + cos * im] if turn else [re, im]
            stacked = jnp.concatenate(blocks, 0)
            for level in range(2):
                corr = corr + jnp.dot(
                    tables[which][level], stacked, preferred_element_type=jnp.float32
                )
        corr = corr * (scale * (1 - 2 * (side * rho % 2)).astype(jnp.float32))
        peak = corr[:, :WCOLS]
        power = corr[:, :WCOLS] * corr[:, :WCOLS]
        for start in range(WCOLS, wide, WCOLS):
            more = corr[:, start : start + WCOLS]
            peak = jnp.maximum(peak, more)
            power = power + more * more
        shift = group
        while shift < WCOLS:
            peak = jnp.maximum(peak, pltpu.roll(peak, shift, 1))
            power = power + pltpu.roll(power, shift, 1)
            shift *= 2
        if share != 1.0:
            power = power * share
        packed = peak[:height]
        for k in range(1, members):
            source = (power if k % 2 else peak)[k // 2 * height : (k // 2 + 1) * height]
            packed = jnp.where(kappa == k, source, packed)
        outs[which][...] = packed.astype(outs[which].dtype)


def columns(parts, tables, group_of, classes, band, scale, share, dtype):
    members = len(parts) // 2
    many = len(group_of)
    steps = tables[0].shape[1]
    height = steps // (members // 2)
    width = parts[0].shape[1]
    roots = np.round(np.exp(2j * np.pi * np.arange(classes) / classes), 12)
    roots = jnp.asarray(np.stack([roots.real, roots.imag]).astype(np.float32))
    return pl.pallas_call(
        functools.partial(column_kernel, group_of, scale, share),
        out_shape=[jax.ShapeDtypeStruct((height, WCOLS), dtype)] * many,
        in_specs=[SMEM] + vmem(many + 2 * members),
        out_specs=vmem(many),
        scratch_shapes=[
            pltpu.VMEM((members, band, width), jnp.bfloat16),
            pltpu.VMEM((members, PAD, width), jnp.bfloat16),
        ],
        compiler_params=params(COLUMN_MB),
        cost_estimate=pl.CostEstimate(
            flops=many * 2 * tables[0].size * width // 2,
            bytes_accessed=2 * many * tables[0].size,
            transcendentals=0,
        ),
        name="columns",
    )(roots, *tables, *parts)


def unpack_kernel(classes, *rest):
    near = rest[:classes]
    far = rest[classes : 2 * classes]
    peak_ref, power_ref = rest[2 * classes :]
    row, core, members, _, side = place()
    half = classes // 2
    height = near[0].shape[0]
    group = WCOLS // members
    lane_group = lax.broadcasted_iota(jnp.int32, (height, WCOLS), 1) // group
    for delta in range(2):
        mic = lax.bitwise_xor(side, delta)
        for k in range(members):
            wanted = (lane_group + (members - k)) % members
            value = jnp.zeros((height, WCOLS), jnp.float32)
            for low in range(half):
                s = delta * half + low
                base = lax.bitwise_xor(row, s) % half * 2
                for source, at in ((near, core), (far, 1 - core)):
                    value = jnp.where(wanted == base + at, source[s][...].astype(jnp.float32), value)
            if k:
                value = pltpu.roll(value, WCOLS - k * group, 1)
            target = power_ref if k % 2 else peak_ref
            target[mic, 0, k // 2 * height : (k // 2 + 1) * height, :] = value


def unpack(near, far, steps):
    classes = len(near)
    shape = jax.ShapeDtypeStruct((2, 1, steps, WCOLS), jnp.float32)
    return pl.pallas_call(
        functools.partial(unpack_kernel, classes),
        out_shape=[shape, shape],
        in_specs=vmem(2 * classes),
        out_specs=vmem(2),
        compiler_params=params(8),
        name="unpack",
    )(*near, *far)


def shards(spectra, bank, orient_index):
    length = spectra.shape[3]
    tsize = bank.shape[1]
    classes = lax.axis_size("row")
    cores = lax.axis_size("orient")
    count = classes * cores
    members = count // 2
    band = length // count
    steps = length // classes
    win = 1 << (tsize + WCOLS - 2).bit_length()
    lanes = win // (length // win)
    line = ("row", "orient")
    window = orient_index.shape[0]
    rows = band // 2

    row = lax.axis_index("row")
    window_tables = jnp.asarray(
        np.stack([window_table(length, win, True), window_table(length, win, False)])
    )
    back = jnp.asarray(back_table(win, lanes))
    flip = flip_table(band)

    opposite = [(i, count - 1 - i) for i in range(count)]
    cos, sin = phases(np.arange(length + PAD), np.arange(tsize), length)
    left = jnp.asarray(np.stack([cos, -sin]).astype(BF16))
    sent = window_first(spectra, window_tables, rows)
    others = [lax.ppermute(sent, line, opposite)]
    spectra, bank, _ = lax.optimization_barrier((spectra, bank, sent))
    sent, keep, *left = window_rest(spectra, window_tables, left, rows)
    others.insert(0, lax.ppermute(sent, line, opposite))
    bank, keep, *left = lax.optimization_barrier((bank, keep, *left))
    lows, highs = [], []
    for block, got in ((0, lows), (1, highs)):
        tspec, *fresh = template_spectra(
            bank, orient_index, left[block], win, lanes, jnp.float32, block == 0
        )
        parts = partials(
            keep,
            others[1 - block :],
            block * rows,
            jnp.asarray(flip[:rows, rows:] if block == 0 else flip[rows:]),
            tspec,
            back,
            members,
            window,
        )
        got.append(parts[0])
        for s in range(1, members):
            got.append(lax.ppermute(parts[s], line, [(i, i ^ s) for i in range(count)]))
        if block == 0:
            bank, left[1], _ = lax.optimization_barrier((fresh[0], left[1], parts[0]))
            early = lows[1 : members // 2 + 1]
            others[0], *early = lax.optimization_barrier((others[0], *early))
            lows[1 : members // 2 + 1] = early

    all_tables = jnp.asarray(column_table(length, classes, cores, band))
    row, _ = lax.optimization_barrier((row, parts[0]))
    maps = [None] * classes
    for group in (range(classes // 2, classes), range(classes // 2)):
        rhos = [reverse_bits(lax.bitwise_xor(row, s), bits(classes)) for s in group]
        made = columns(
            lows + highs,
            [lax.dynamic_index_in_dim(all_tables, rho, 0, False) for rho in rhos],
            tuple(group),
            classes,
            band,
            1.0 / (length * tsize),
            window / max(window, members),
            jnp.bfloat16,
        )
        for s, one in zip(group, made):
            maps[s] = one
    near = [maps[0]]
    for s in range(1, classes):
        near.append(lax.ppermute(maps[s], "row", [(i, i ^ s) for i in range(classes)]))
    far = [lax.ppermute(m, "orient", [(0, 1), (1, 0)]) for m in near]
    peak, power = unpack(near, far, steps)
    return peak, power


def solution(mesh):
    return jax.shard_map(
        shards,
        mesh=mesh,
        in_specs=(P(("grp", "mic"), None, "row", None), P(), P("grp")),
        out_specs=(P(("grp", "mic"), "row", None, None), P(("grp", "mic"), "row", None, None)),
        check_vma=False,
    )
```

```python
import functools
import math

import jax
import jax.numpy as jnp
import ml_dtypes
import numpy as np
from jax import lax
from jax.experimental import pallas as pl
from jax.experimental.pallas import tpu as pltpu
from jax.sharding import PartitionSpec as P

WCOLS = 128
WINDOW_MB = 57
TEMPLATE_MB = 16
PARTIAL_MB = 16
COLUMN_MB = 12
PAD = 16

two_pi = 2.0 * math.pi
BF16 = ml_dtypes.bfloat16


def params(mebibytes):
    return pltpu.CompilerParams(vmem_limit_bytes=mebibytes * 1024 * 1024)


def bits(count):
    return count.bit_length() - 1


def reverse_bits(number, digits):
    result = number * 0
    for digit in range(digits):
        result = result + number // (1 << digit) % 2 * (1 << digits - 1 - digit)
    return result


def phases(rows, cols, period):
    angles = np.outer(rows, cols) % period * (two_pi / period)
    return np.cos(angles), np.sin(angles)


def window_table(length, win, mirrored):
    ratio = length // win
    lanes = win // ratio
    sign = 1 if mirrored else -1
    base = np.arange(win)[:, None] + sign * ratio * np.arange(lanes)[None, :]
    d = (length // ratio * np.arange(ratio)[:, None, None] + base[None]) % length
    u = np.arange(win)
    kernel = np.exp(2j * np.pi * (np.outer(np.arange(length), u) % length) / length).sum(1) / win
    val = kernel[d]
    return np.concatenate([val.real, val.imag], 2).astype(BF16)


def tiles_of(re, im, lanes, axis):
    pieces = []
    for start in range(0, re.shape[axis], lanes):
        cut = [slice(None)] * re.ndim
        cut[axis] = slice(start, start + lanes)
        pieces += [re[tuple(cut)], im[tuple(cut)]]
    return np.concatenate(pieces, axis)


def template_table(tsize, win, lanes):
    cos, sin = phases(np.arange(tsize), np.arange(win), win)
    upper = tiles_of(cos, -sin, lanes, 1)
    lower = tiles_of(sin, cos, lanes, 1)
    return np.concatenate([upper, lower], 0).astype(BF16)


def split(table):
    upper = table.astype(BF16)
    return np.stack([upper, (table - upper.astype(np.float64)).astype(BF16)])


def back_table(win, lanes):
    cos, sin = phases(np.arange(win), np.arange(WCOLS), win)
    re_rows = np.concatenate([cos, sin], 1)
    im_rows = np.concatenate([-sin, cos], 1)
    table = tiles_of(re_rows, im_rows, lanes, 0)
    return split(table.reshape(win // lanes, 2 * lanes, 2 * WCOLS))


def sorted_rows(count):
    return np.concatenate([np.arange(0, count, 2), np.arange(1, count, 2)])


def column_table(length, classes, cores, band):
    steps = length // classes
    freqs = np.arange(cores * band)
    out = []
    for rho in range(classes):
        rows = rho + classes * np.arange(steps // 2)
        for parity in range(2):
            cos, sin = phases(rows, freqs[parity::2], length)
            upper, lower = split(tiles_of(cos, -sin, band // 2, 1))
            out.append(np.concatenate([upper, lower], 0))
    return np.stack(out).reshape(classes, 2, steps, cores * band)


def flip_table(band):
    out = np.zeros((band + PAD, band), np.float32)
    out[band - np.arange(band), np.arange(band)] = 1.0
    return out.astype(BF16)


def vmem(count):
    return [pl.BlockSpec(memory_space=pltpu.VMEM)] * count


def hbm(count):
    return [pl.BlockSpec(memory_space=pltpu.HBM)] * count


SMEM = pl.BlockSpec(memory_space=pltpu.SMEM)


def place():
    row, core = lax.axis_index("row"), lax.axis_index("orient")
    cores = lax.axis_size("orient")
    members = lax.axis_size("row") * cores // 2
    device = row * cores + core
    return row, core, members, device % members, device // members


def window_block(mirrored, spec, table, out_ref, order=None):
    rows, total = out_ref.shape
    ratio = table(None)
    width = total // ratio
    lanes = width // 2
    win = ratio * lanes
    pieces = []
    for step in range(ratio):
        at = slice(step * win, (step + 1) * win)
        pieces += [spec(part, at) for part in range(2)]
    stacked = jnp.concatenate(pieces, 0)
    got = [
        jnp.dot(stacked, table(which), preferred_element_type=jnp.float32)
        for which in range(ratio)
    ]
    for part in range(ratio):
        re, im = 0.0, 0.0
        for which in range(ratio):
            step = (which - part if mirrored else which + part) % ratio
            re = re + got[which][2 * step * rows : (2 * step + 1) * rows]
            im = im + got[which][(2 * step + 1) * rows : (2 * step + 2) * rows]
        out_re = re[:, :lanes] - im[:, lanes:]
        out_im = re[:, lanes:] + im[:, :lanes]
        if mirrored:
            out_im = -out_im
        both = jnp.concatenate([out_re, out_im], 1)
        if order is not None:
            upper = both.astype(jnp.bfloat16)
            lower = (both - upper.astype(jnp.float32)).astype(jnp.bfloat16)
            both = jnp.dot(order, upper, preferred_element_type=jnp.float32)
            both += jnp.dot(order, lower, preferred_element_type=jnp.float32)
        out_ref[:, part * width : (part + 1) * width] = both.astype(out_ref.dtype)


def first_kernel(spec_ref, tables_ref, out_ref, held_ref, table_ref, sem):
    rows = out_ref.shape[0]
    _, core, _, _, side = place()
    start = pl.multiple_of((2 * core + 1) * rows, rows)
    copies = [
        pltpu.make_async_copy(
            spec_ref.at[1 - side, :, pl.ds(start, rows)], held_ref, sem.at[0]
        ),
        pltpu.make_async_copy(tables_ref.at[0], table_ref, sem.at[1]),
    ]
    for copy in copies:
        copy.start()
    for copy in copies:
        copy.wait()
    window_block(
        True,
        lambda part, at: held_ref[part, :, at],
        lambda k: table_ref.shape[0] if k is None else table_ref[k],
        out_ref,
    )


def window_first(spectra, tables, rows):
    _, ratio, win, width = tables.shape
    return pl.pallas_call(
        first_kernel,
        out_shape=jax.ShapeDtypeStruct((rows, ratio * width), jnp.bfloat16),
        in_specs=hbm(2),
        out_specs=vmem(1)[0],
        scratch_shapes=[
            pltpu.VMEM((2, rows, ratio * win), jnp.bfloat16),
            pltpu.VMEM((ratio, win, width), jnp.bfloat16),
            pltpu.SemaphoreType.DMA((2,)),
        ],
        compiler_params=params(WINDOW_MB),
        cost_estimate=pl.CostEstimate(
            flops=4 * rows * ratio * win * ratio * width,
            bytes_accessed=8 * rows * ratio * win,
            transcendentals=0,
        ),
        name="window_first",
    )(spectra, tables)


def rest_kernel(place_ref, spec_ref, table_ref, order_ref, main_ref, more_ref, *outs):
    sent_ref, keep_ref, low_ref, high_ref = outs
    step = pl.program_id(0)
    spec = lambda part, at: spec_ref[0, part, :, at]
    table = lambda k: table_ref.shape[1] if k is None else table_ref[0, k]

    @pl.when(step == 0)
    def _():
        window_block(True, spec, table, sent_ref)
        low, band = low_ref.shape[1], main_ref.shape[1]
        low_ref[...] = main_ref[:, :low]
        high_ref[:, : band - low] = main_ref[:, low:]
        high_ref[:, band - low :] = more_ref[...]

    @pl.when(step > 0)
    def _():
        window_block(False, spec, table, keep_ref, order_ref[...])


def window_rest(spectra, tables, left, rows):
    _, ratio, win, width = tables.shape
    row, core, members, _, side = place()
    device = row * lax.axis_size("orient") + core
    band = 2 * rows
    tsize = left.shape[2]
    at = jnp.stack([side, core, device]).astype(jnp.int32)
    order = jnp.asarray(np.eye(rows)[sorted_rows(rows)].astype(BF16))

    def spec_index(i, at):
        first = jnp.where(i == 0, 1, 0)
        return at[0] + first * (1 - 2 * at[0]), 0, 2 * at[1] + jnp.maximum(i - 1, 0), 0

    return pl.pallas_call(
        rest_kernel,
        out_shape=[
            jax.ShapeDtypeStruct((rows, ratio * width), jnp.bfloat16),
            jax.ShapeDtypeStruct((band, ratio * width), jnp.float32),
            jax.ShapeDtypeStruct((2, rows, tsize), jnp.bfloat16),
            jax.ShapeDtypeStruct((2, rows + PAD, tsize), jnp.bfloat16),
        ],
        grid_spec=pltpu.PrefetchScalarGridSpec(
            num_scalar_prefetch=1,
            grid=(3,),
            in_specs=[
                pl.BlockSpec((1, 2, rows, ratio * win), spec_index),
                pl.BlockSpec((1, ratio, win, width), lambda i, at: (jnp.minimum(i, 1), 0, 0, 0)),
                pl.BlockSpec((rows, rows), lambda i, at: (0, 0)),
                pl.BlockSpec((2, band, tsize), lambda i, at: (0, at[2], 0)),
                pl.BlockSpec((2, PAD, tsize), lambda i, at: (0, (at[2] + 1) * (band // PAD), 0)),
            ],
            out_specs=[
                pl.BlockSpec((rows, ratio * width), lambda i, at: (0, 0)),
                pl.BlockSpec((rows, ratio * width), lambda i, at: (jnp.maximum(i - 1, 0), 0)),
                pl.BlockSpec((2, rows, tsize), lambda i, at: (0, 0, 0)),
                pl.BlockSpec((2, rows + PAD, tsize), lambda i, at: (0, 0, 0)),
            ],
        ),
        compiler_params=params(WINDOW_MB),
        cost_estimate=pl.CostEstimate(
            flops=12 * rows * ratio * win * ratio * width,
            bytes_accessed=20 * rows * ratio * win,
            transcendentals=0,
        ),
        name="window_rest",
    )(at, spectra, tables, order, left, left)


def template_kernel(fresh, index_ref, bank_ref, left_ref, right_ref, out_ref, *rest):
    hold_ref = rest[-1]
    ratio, depth, width = right_ref.shape
    window, rows = hold_ref.shape[0], hold_ref.shape[1]
    left = jnp.concatenate([left_ref[0], left_ref[1]], 0)
    for o in range(window):
        if fresh:
            values = bank_ref[index_ref[o]].astype(jnp.float32)
            share = 1.0 / values.size
            total = jnp.sum(jnp.sum(values, 0, keepdims=True), 1, keepdims=True)
            centred = values - total * share
            square = jnp.sum(jnp.sum(centred * centred, 0, keepdims=True), 1, keepdims=True)
            factor = lax.rsqrt(square * share + 1e-06)
            template = (centred * factor).astype(jnp.bfloat16)
            rest[0][o] = template
        else:
            template = bank_ref[o]
        rowpass = jnp.dot(left, template, preferred_element_type=jnp.float32).astype(jnp.bfloat16)
        hold_ref[o] = jnp.concatenate([rowpass[:rows], rowpass[rows:]], 1)
    flat = hold_ref[...].reshape(window * rows, depth)
    for part in range(ratio):
        got = jnp.dot(flat, right_ref[part], preferred_element_type=jnp.float32)
        out_ref[part] = got.astype(out_ref.dtype)


def template_spectra(bank, orient_index, left, win, lanes, dtype, fresh):
    tsize = bank.shape[1]
    window = orient_index.shape[0]
    ratio = win // lanes
    rows = left.shape[1]
    right = template_table(tsize, win, lanes).reshape(2 * tsize, ratio, 2 * lanes)
    right = jnp.asarray(np.ascontiguousarray(right.transpose(1, 0, 2)))
    out_shape = [jax.ShapeDtypeStruct((ratio, window * rows, 2 * lanes), dtype)]
    if fresh:
        out_shape.append(jax.ShapeDtypeStruct((window, tsize, tsize), jnp.bfloat16))
    return pl.pallas_call(
        functools.partial(template_kernel, fresh),
        out_shape=out_shape,
        in_specs=[SMEM] + vmem(3),
        out_specs=vmem(len(out_shape)),
        scratch_shapes=[pltpu.VMEM((window, rows, 2 * tsize), jnp.bfloat16)],
        compiler_params=params(TEMPLATE_MB),
        cost_estimate=pl.CostEstimate(
            flops=2 * window * rows * tsize * (2 * tsize + 4 * win),
            bytes_accessed=2 * bank.size + 4 * window * rows * 2 * win,
            transcendentals=0,
        ),
        name="templates",
    )(orient_index, bank, left, right)


def partial_kernel(count, first, keep_ref, flip_ref, tspec_ref, back_ref, *rest):
    other_refs, rest = rest[:count], rest[count:]
    part_ref, outs = rest[-1], rest[:-1]
    _, _, members, mine, _ = place()
    window = part_ref.shape[0]
    band = keep_ref.shape[0] // 2
    rows = flip_ref.shape[0]
    ratio, _, width = tspec_ref.shape
    lanes = width // 2
    received = jnp.concatenate([other[...] for other in other_refs], 0)
    held = jnp.dot(flip_ref[...], received, preferred_element_type=jnp.float32)
    head = held[:band] + keep_ref[first : first + band]
    held = head if rows == band else jnp.concatenate([head, held[band:]], 0)
    total = None
    for part in range(ratio):
        mic_re = held[:, part * width : part * width + lanes]
        mic_im = held[:, part * width + lanes : (part + 1) * width]
        upper, lower = [], []
        for o in range(window):
            tmpl_re = tspec_ref[part, o * rows : (o + 1) * rows, :lanes].astype(jnp.float32)
            tmpl_im = tspec_ref[part, o * rows : (o + 1) * rows, lanes:].astype(jnp.float32)
            prod_re = mic_re * tmpl_re + mic_im * tmpl_im
            prod_im = mic_im * tmpl_re - mic_re * tmpl_im
            product = jnp.concatenate([prod_re, prod_im], 1)
            rounded = product.astype(jnp.bfloat16)
            upper.append(rounded)
            lower.append((product - rounded.astype(jnp.float32)).astype(jnp.bfloat16))
        upper = jnp.concatenate(upper, 0)
        lower = jnp.concatenate(lower, 0)
        got = jnp.dot(upper, back_ref[0, part], preferred_element_type=jnp.float32)
        got += jnp.dot(lower, back_ref[0, part], preferred_element_type=jnp.float32)
        got += jnp.dot(upper, back_ref[1, part], preferred_element_type=jnp.float32)
        total = got if total is None else total + got
    for o in range(window):
        part_ref[o] = total[o * rows : (o + 1) * rows]

    group = WCOLS // members
    lane_group = lax.broadcasted_iota(jnp.int32, (rows, WCOLS), 1) // group
    tiles = max(1, window // members)
    for tile in range(tiles):
        for plane in range(2):
            at = slice(plane * WCOLS, (plane + 1) * WCOLS)
            pieces = []
            for i in range(members):
                piece = part_ref[(tile * members + i) % window, :, at]
                pieces.append(pltpu.roll(piece, group * i, 1) if i else piece)
            for s in range(members):
                target = lax.bitwise_xor(mine, s)
                packed = pieces[0]
                for i in range(1, members):
                    inside = (lane_group + (members - i)) % members == target
                    packed = jnp.where(inside, pieces[i], packed)
                start = (plane * tiles + tile) * WCOLS
                outs[s][:, start : start + WCOLS] = packed.astype(outs[s].dtype)


def partials(keep, others, first, flip, tspec, back, members, window):
    rows = flip.shape[0]
    ratio, _, width = tspec.shape
    tiles = max(1, window // members)
    out_shape = (rows, 2 * tiles * WCOLS)
    return pl.pallas_call(
        functools.partial(partial_kernel, len(others), first),
        out_shape=[jax.ShapeDtypeStruct(out_shape, jnp.bfloat16)] * members,
        in_specs=vmem(4 + len(others)),
        out_specs=vmem(members),
        scratch_shapes=[
            pltpu.VMEM((window, rows, 2 * WCOLS), jnp.float32),
        ],
        compiler_params=params(PARTIAL_MB),
        cost_estimate=pl.CostEstimate(
            flops=12 * tspec.size * WCOLS,
            bytes_accessed=2 * tspec.size,
            transcendentals=0,
        ),
        name="partials",
    )(keep, flip, tspec, back, *others)


def column_kernel(group_of, scale, share, roots_ref, *rest):
    row, core, members, mine, side = place()
    cores, classes = lax.axis_size("orient"), lax.axis_size("row")
    many = len(group_of)
    tables, rest = rest[:many], rest[many:]
    low_parts, high_parts = rest[:members], rest[members : 2 * members]
    outs = rest[2 * members : 2 * members + many]
    held_ref, last_ref = rest[2 * members + many :]
    _, steps, depth = tables[0].shape
    low, width = low_parts[0].shape
    band = held_ref.shape[1]
    wide = width // 2
    for s in range(members):
        member = lax.bitwise_xor(mine, s)
        held_ref[member, :low] = low_parts[s][...]
        held_ref[member, low:] = high_parts[s][: band - low]
        last_ref[member] = high_parts[s][band - low :]
    planes = [[], []]
    for member in range(members):
        block = held_ref[member]
        for parity in range(2):
            at = parity * (low // 2)
            piece = jnp.concatenate(
                [block[at : at + low // 2], block[low + at : low + at + low // 2]], 0
            )
            if member and not parity:
                head = piece[:PAD].astype(jnp.float32) + last_ref[member - 1].astype(jnp.float32)
                piece = jnp.concatenate([head.astype(jnp.bfloat16), piece[PAD:]], 0)
            planes[parity].append((piece[:, :wide], piece[:, wide:]))
    top = last_ref[members - 1][:1, :wide].astype(jnp.float32)
    group = WCOLS // members
    height = steps // (members // 2)
    lane_group = lax.broadcasted_iota(jnp.int32, (height, WCOLS), 1) // group
    kappa = (lane_group + (members - mine)) % members
    for which in range(many):
        rho = reverse_bits(lax.bitwise_xor(row, group_of[which]), bits(classes))
        sums = [(1 - 2 * (rho % 2)).astype(jnp.float32) * top, 0.0]
        for parity in range(2):
            for turn in range(members // cores):
                angle = rho * turn % classes
                cos = roots_ref[0, angle].astype(jnp.bfloat16)
                sin = roots_ref[1, angle].astype(jnp.bfloat16)
                blocks = []
                for re, im in planes[parity][turn * cores : (turn + 1) * cores]:
                    blocks += [cos * re - sin * im, sin * re + cos * im] if turn else [re, im]
                stacked = jnp.concatenate(blocks, 0)
                got = jnp.dot(tables[which][parity], stacked, preferred_element_type=jnp.float32)
                sums[parity] = sums[parity] + got[: steps // 2] + got[steps // 2 :]
        corr = jnp.concatenate([sums[0] + sums[1], sums[0] - sums[1]], 0)
        corr = corr * (scale * (1 - 2 * (side * rho % 2)).astype(jnp.float32))
        peak = corr[:, :WCOLS]
        power = corr[:, :WCOLS] * corr[:, :WCOLS]
        for start in range(WCOLS, wide, WCOLS):
            more = corr[:, start : start + WCOLS]
            peak = jnp.maximum(peak, more)
            power = power + more * more
        shift = group
        while shift < WCOLS:
            peak = jnp.maximum(peak, pltpu.roll(peak, shift, 1))
            power = power + pltpu.roll(power, shift, 1)
            shift *= 2
        if share != 1.0:
            power = power * share
        packed = peak[:height]
        for k in range(1, members):
            source = (power if k % 2 else peak)[k // 2 * height : (k // 2 + 1) * height]
            packed = jnp.where(kappa == k, source, packed)
        outs[which][...] = packed.astype(outs[which].dtype)


def columns(parts, tables, group_of, classes, band, scale, share, dtype):
    members = len(parts) // 2
    many = len(group_of)
    steps = tables[0].shape[1]
    height = steps // (members // 2)
    width = parts[0].shape[1]
    roots = np.round(np.exp(2j * np.pi * np.arange(classes) / classes), 12)
    roots = jnp.asarray(np.stack([roots.real, roots.imag]).astype(np.float32))
    return pl.pallas_call(
        functools.partial(column_kernel, group_of, scale, share),
        out_shape=[jax.ShapeDtypeStruct((height, WCOLS), dtype)] * many,
        in_specs=[SMEM] + vmem(many + 2 * members),
        out_specs=vmem(many),
        scratch_shapes=[
            pltpu.VMEM((members, band, width), jnp.bfloat16),
            pltpu.VMEM((members, PAD, width), jnp.bfloat16),
        ],
        compiler_params=params(COLUMN_MB),
        cost_estimate=pl.CostEstimate(
            flops=many * 2 * tables[0].size * width // 2,
            bytes_accessed=2 * many * tables[0].size,
            transcendentals=0,
        ),
        name="columns",
    )(roots, *tables, *parts)


def unpack_kernel(classes, *rest):
    near = rest[:classes]
    far = rest[classes : 2 * classes]
    peak_ref, power_ref = rest[2 * classes :]
    row, core, members, _, side = place()
    half = classes // 2
    height = near[0].shape[0]
    group = WCOLS // members
    lane_group = lax.broadcasted_iota(jnp.int32, (height, WCOLS), 1) // group
    for delta in range(2):
        mic = lax.bitwise_xor(side, delta)
        for k in range(members):
            wanted = (lane_group + (members - k)) % members
            value = jnp.zeros((height, WCOLS), jnp.float32)
            for low in range(half):
                s = delta * half + low
                base = lax.bitwise_xor(row, s) % half * 2
                for source, at in ((near, core), (far, 1 - core)):
                    value = jnp.where(wanted == base + at, source[s][...].astype(jnp.float32), value)
            if k:
                value = pltpu.roll(value, WCOLS - k * group, 1)
            target = power_ref if k % 2 else peak_ref
            target[mic, 0, k // 2 * height : (k // 2 + 1) * height, :] = value


def unpack(near, far, steps):
    classes = len(near)
    shape = jax.ShapeDtypeStruct((2, 1, steps, WCOLS), jnp.float32)
    return pl.pallas_call(
        functools.partial(unpack_kernel, classes),
        out_shape=[shape, shape],
        in_specs=vmem(2 * classes),
        out_specs=vmem(2),
        compiler_params=params(8),
        name="unpack",
    )(*near, *far)


def shards(spectra, bank, orient_index):
    length = spectra.shape[3]
    tsize = bank.shape[1]
    classes = lax.axis_size("row")
    cores = lax.axis_size("orient")
    count = classes * cores
    members = count // 2
    band = length // count
    steps = length // classes
    win = 1 << (tsize + WCOLS - 2).bit_length()
    lanes = win // (length // win)
    line = ("row", "orient")
    window = orient_index.shape[0]
    rows = band // 2

    row = lax.axis_index("row")
    window_tables = jnp.asarray(
        np.stack([window_table(length, win, True), window_table(length, win, False)])
    )
    back = jnp.asarray(back_table(win, lanes))
    flip = flip_table(band)
    order = sorted_rows(rows)
    flips = [flip[:rows, rows:][order], np.concatenate([flip[rows:band][order], flip[band:]], 0)]

    opposite = [(i, count - 1 - i) for i in range(count)]
    cos, sin = phases(np.arange(length + PAD), np.arange(tsize), length)
    left = np.stack([cos, -sin]).astype(BF16)
    chunked = left[:, :length].reshape(2, -1, rows, tsize)[:, :, sorted_rows(rows)]
    left = jnp.asarray(np.concatenate([chunked.reshape(2, length, tsize), left[:, length:]], 1))
    sent = window_first(spectra, window_tables, rows)
    others = [lax.ppermute(sent, line, opposite)]
    spectra, bank, _ = lax.optimization_barrier((spectra, bank, sent))
    sent, keep, *left = window_rest(spectra, window_tables, left, rows)
    others.insert(0, lax.ppermute(sent, line, opposite))
    bank, keep, *left = lax.optimization_barrier((bank, keep, *left))
    lows, highs = [], []
    for block, got in ((0, lows), (1, highs)):
        tspec, *fresh = template_spectra(
            bank, orient_index, left[block], win, lanes, jnp.float32, block == 0
        )
        parts = partials(
            keep,
            others[1 - block :],
            block * rows,
            jnp.asarray(flips[block]),
            tspec,
            back,
            members,
            window,
        )
        got.append(parts[0])
        for s in range(1, members):
            got.append(lax.ppermute(parts[s], line, [(i, i ^ s) for i in range(count)]))
        if block == 0:
            bank, left[1], _ = lax.optimization_barrier((fresh[0], left[1], parts[0]))
            early = lows[1 : members // 2 + 1]
            others[0], *early = lax.optimization_barrier((others[0], *early))
            lows[1 : members // 2 + 1] = early

    all_tables = jnp.asarray(column_table(length, classes, cores, band))
    row, _ = lax.optimization_barrier((row, parts[0]))
    maps = [None] * classes
    for group in (range(classes // 2, classes), range(classes // 2)):
        rhos = [reverse_bits(lax.bitwise_xor(row, s), bits(classes)) for s in group]
        made = columns(
            lows + highs,
            [lax.dynamic_index_in_dim(all_tables, rho, 0, False) for rho in rhos],
            tuple(group),
            classes,
            band,
            1.0 / (length * tsize),
            window / max(window, members),
            jnp.bfloat16,
        )
        for s, one in zip(group, made):
            maps[s] = one
    near = [maps[0]]
    for s in range(1, classes):
        near.append(lax.ppermute(maps[s], "row", [(i, i ^ s) for i in range(classes)]))
    far = [lax.ppermute(m, "orient", [(0, 1), (1, 0)]) for m in near]
    peak, power = unpack(near, far, steps)
    return peak, power


def solution(mesh):
    return jax.shard_map(
        shards,
        mesh=mesh,
        in_specs=(P(("grp", "mic"), None, "row", None), P(), P("grp")),
        out_specs=(P(("grp", "mic"), "row", None, None), P(("grp", "mic"), "row", None, None)),
        check_vma=False,
    )
```

```python
import functools
import math

import jax
import jax.numpy as jnp
import ml_dtypes
import numpy as np
from jax import lax
from jax.experimental import pallas as pl
from jax.experimental.pallas import tpu as pltpu
from jax.sharding import PartitionSpec as P

WCOLS = 128
WINDOW_MB = 57
TEMPLATE_MB = 16
PARTIAL_MB = 16
COLUMN_MB = 12
PAD = 16

two_pi = 2.0 * math.pi
BF16 = ml_dtypes.bfloat16


def params(mebibytes):
    return pltpu.CompilerParams(vmem_limit_bytes=mebibytes * 1024 * 1024)


def bits(count):
    return count.bit_length() - 1


def reverse_bits(number, digits):
    result = number * 0
    for digit in range(digits):
        result = result + number // (1 << digit) % 2 * (1 << digits - 1 - digit)
    return result


def phases(rows, cols, period):
    angles = np.outer(rows, cols) % period * (two_pi / period)
    return np.cos(angles), np.sin(angles)


def window_table(length, win, mirrored):
    ratio = length // win
    lanes = win // ratio
    sign = 1 if mirrored else -1
    base = np.arange(win)[:, None] + sign * ratio * np.arange(lanes)[None, :]
    d = (length // ratio * np.arange(ratio)[:, None, None] + base[None]) % length
    u = np.arange(win)
    kernel = np.exp(2j * np.pi * (np.outer(np.arange(length), u) % length) / length).sum(1) / win
    val = kernel[d]
    return np.concatenate([val.real, val.imag], 2).astype(BF16)


def tiles_of(re, im, lanes, axis):
    pieces = []
    for start in range(0, re.shape[axis], lanes):
        cut = [slice(None)] * re.ndim
        cut[axis] = slice(start, start + lanes)
        pieces += [re[tuple(cut)], im[tuple(cut)]]
    return np.concatenate(pieces, axis)


def template_table(tsize, win, lanes):
    cos, sin = phases(np.arange(tsize), np.arange(win), win)
    upper = tiles_of(cos, -sin, lanes, 1)
    lower = tiles_of(sin, cos, lanes, 1)
    return np.concatenate([upper, lower], 0).astype(BF16)


def split(table):
    upper = table.astype(BF16)
    return np.stack([upper, (table - upper.astype(np.float64)).astype(BF16)])


def back_table(win, lanes):
    cos, sin = phases(np.arange(win), np.arange(WCOLS), win)
    re_rows = np.concatenate([cos, sin], 1)
    im_rows = np.concatenate([-sin, cos], 1)
    table = tiles_of(re_rows, im_rows, lanes, 0)
    return split(table.reshape(win // lanes, 2 * lanes, 2 * WCOLS))


def sorted_rows(count):
    return np.concatenate([np.arange(0, count, 2), np.arange(1, count, 2)])


def column_table(length, classes, cores, band):
    steps = length // classes
    freqs = np.arange(cores * band)
    out = []
    for rho in range(classes):
        rows = rho + classes * np.arange(steps // 2)
        for parity in range(2):
            cos, sin = phases(rows, freqs[parity::2], length)
            upper, lower = split(tiles_of(cos, -sin, band // 2, 1))
            out.append(np.concatenate([upper, lower], 0))
    return np.stack(out).reshape(classes, 2, steps, cores * band)


def flip_table(band):
    out = np.zeros((band + PAD, band), np.float32)
    out[band - np.arange(band), np.arange(band)] = 1.0
    return out.astype(BF16)


def vmem(count):
    return [pl.BlockSpec(memory_space=pltpu.VMEM)] * count


def hbm(count):
    return [pl.BlockSpec(memory_space=pltpu.HBM)] * count


SMEM = pl.BlockSpec(memory_space=pltpu.SMEM)


def place():
    row, core = lax.axis_index("row"), lax.axis_index("orient")
    cores = lax.axis_size("orient")
    members = lax.axis_size("row") * cores // 2
    device = row * cores + core
    return row, core, members, device % members, device // members


def window_block(mirrored, spec, table, out_ref, order=None):
    rows, total = out_ref.shape
    ratio = table(None)
    width = total // ratio
    lanes = width // 2
    win = ratio * lanes
    pieces = []
    for step in range(ratio):
        at = slice(step * win, (step + 1) * win)
        pieces += [spec(part, at) for part in range(2)]
    stacked = jnp.concatenate(pieces, 0)
    got = [
        jnp.dot(stacked, table(which), preferred_element_type=jnp.float32)
        for which in range(ratio)
    ]
    for part in range(ratio):
        re, im = 0.0, 0.0
        for which in range(ratio):
            step = (which - part if mirrored else which + part) % ratio
            re = re + got[which][2 * step * rows : (2 * step + 1) * rows]
            im = im + got[which][(2 * step + 1) * rows : (2 * step + 2) * rows]
        out_re = re[:, :lanes] - im[:, lanes:]
        out_im = re[:, lanes:] + im[:, :lanes]
        if mirrored:
            out_im = -out_im
        both = jnp.concatenate([out_re, out_im], 1)
        if order is not None:
            upper = both.astype(jnp.bfloat16)
            lower = (both - upper.astype(jnp.float32)).astype(jnp.bfloat16)
            both = jnp.dot(order, upper, preferred_element_type=jnp.float32)
            both += jnp.dot(order, lower, preferred_element_type=jnp.float32)
        out_ref[:, part * width : (part + 1) * width] = both.astype(out_ref.dtype)


def first_kernel(spec_ref, tables_ref, out_ref, held_ref, table_ref, sem):
    rows = out_ref.shape[0]
    _, core, _, _, side = place()
    start = pl.multiple_of((2 * core + 1) * rows, rows)
    copies = [
        pltpu.make_async_copy(
            spec_ref.at[1 - side, :, pl.ds(start, rows)], held_ref, sem.at[0]
        ),
        pltpu.make_async_copy(tables_ref.at[0], table_ref, sem.at[1]),
    ]
    for copy in copies:
        copy.start()
    for copy in copies:
        copy.wait()
    window_block(
        True,
        lambda part, at: held_ref[part, :, at],
        lambda k: table_ref.shape[0] if k is None else table_ref[k],
        out_ref,
    )


def window_first(spectra, tables, rows):
    _, ratio, win, width = tables.shape
    return pl.pallas_call(
        first_kernel,
        out_shape=jax.ShapeDtypeStruct((rows, ratio * width), jnp.bfloat16),
        in_specs=hbm(2),
        out_specs=vmem(1)[0],
        scratch_shapes=[
            pltpu.VMEM((2, rows, ratio * win), jnp.bfloat16),
            pltpu.VMEM((ratio, win, width), jnp.bfloat16),
            pltpu.SemaphoreType.DMA((2,)),
        ],
        compiler_params=params(WINDOW_MB),
        cost_estimate=pl.CostEstimate(
            flops=4 * rows * ratio * win * ratio * width,
            bytes_accessed=8 * rows * ratio * win,
            transcendentals=0,
        ),
        name="window_first",
    )(spectra, tables)


def rest_kernel(place_ref, spec_ref, table_ref, order_ref, main_ref, more_ref, *outs):
    sent_ref, keep_ref, low_ref, high_ref = outs
    step = pl.program_id(0)
    spec = lambda part, at: spec_ref[0, part, :, at]
    table = lambda k: table_ref.shape[1] if k is None else table_ref[0, k]

    @pl.when(step == 0)
    def _():
        window_block(True, spec, table, sent_ref)
        low, band = low_ref.shape[1], main_ref.shape[1]
        low_ref[...] = main_ref[:, :low]
        high_ref[:, : band - low] = main_ref[:, low:]
        high_ref[:, band - low :] = more_ref[...]

    @pl.when(step > 0)
    def _():
        window_block(False, spec, table, keep_ref, order_ref[...])


def window_rest(spectra, tables, left, rows):
    _, ratio, win, width = tables.shape
    row, core, members, _, side = place()
    device = row * lax.axis_size("orient") + core
    band = 2 * rows
    tsize = left.shape[2]
    at = jnp.stack([side, core, device]).astype(jnp.int32)
    order = jnp.asarray(np.eye(rows)[sorted_rows(rows)].astype(BF16))

    def spec_index(i, at):
        first = jnp.where(i == 0, 1, 0)
        return at[0] + first * (1 - 2 * at[0]), 0, 2 * at[1] + jnp.maximum(i - 1, 0), 0

    return pl.pallas_call(
        rest_kernel,
        out_shape=[
            jax.ShapeDtypeStruct((rows, ratio * width), jnp.bfloat16),
            jax.ShapeDtypeStruct((band, ratio * width), jnp.float32),
            jax.ShapeDtypeStruct((2, rows, tsize), jnp.bfloat16),
            jax.ShapeDtypeStruct((2, rows + PAD, tsize), jnp.bfloat16),
        ],
        grid_spec=pltpu.PrefetchScalarGridSpec(
            num_scalar_prefetch=1,
            grid=(3,),
            in_specs=[
                pl.BlockSpec((1, 2, rows, ratio * win), spec_index),
                pl.BlockSpec((1, ratio, win, width), lambda i, at: (jnp.minimum(i, 1), 0, 0, 0)),
                pl.BlockSpec((rows, rows), lambda i, at: (0, 0)),
                pl.BlockSpec((2, band, tsize), lambda i, at: (0, at[2], 0)),
                pl.BlockSpec((2, PAD, tsize), lambda i, at: (0, (at[2] + 1) * (band // PAD), 0)),
            ],
            out_specs=[
                pl.BlockSpec((rows, ratio * width), lambda i, at: (0, 0)),
                pl.BlockSpec((rows, ratio * width), lambda i, at: (jnp.maximum(i - 1, 0), 0)),
                pl.BlockSpec((2, rows, tsize), lambda i, at: (0, 0, 0)),
                pl.BlockSpec((2, rows + PAD, tsize), lambda i, at: (0, 0, 0)),
            ],
        ),
        compiler_params=params(WINDOW_MB),
        cost_estimate=pl.CostEstimate(
            flops=12 * rows * ratio * win * ratio * width,
            bytes_accessed=20 * rows * ratio * win,
            transcendentals=0,
        ),
        name="window_rest",
    )(at, spectra, tables, order, left, left)


def template_kernel(fresh, index_ref, bank_ref, left_ref, right_ref, out_ref, *rest):
    hold_ref = rest[-1]
    ratio, depth, width = right_ref.shape
    window, rows = hold_ref.shape[0], hold_ref.shape[1]
    left = jnp.concatenate([left_ref[0], left_ref[1]], 0)
    for o in range(window):
        if fresh:
            values = bank_ref[index_ref[o]].astype(jnp.float32)
            share = 1.0 / values.size
            total = jnp.sum(jnp.sum(values, 0, keepdims=True), 1, keepdims=True)
            centred = values - total * share
            square = jnp.sum(jnp.sum(centred * centred, 0, keepdims=True), 1, keepdims=True)
            factor = lax.rsqrt(square * share + 1e-06)
            template = (centred * factor).astype(jnp.bfloat16)
            rest[0][o] = template
        else:
            template = bank_ref[o]
        rowpass = jnp.dot(left, template, preferred_element_type=jnp.float32).astype(jnp.bfloat16)
        hold_ref[o] = jnp.concatenate([rowpass[:rows], rowpass[rows:]], 1)
    flat = hold_ref[...].reshape(window * rows, depth)
    for part in range(ratio):
        got = jnp.dot(flat, right_ref[part], preferred_element_type=jnp.float32)
        out_ref[part] = got.astype(out_ref.dtype)


def template_spectra(bank, orient_index, left, win, lanes, dtype, fresh):
    tsize = bank.shape[1]
    window = orient_index.shape[0]
    ratio = win // lanes
    rows = left.shape[1]
    right = template_table(tsize, win, lanes).reshape(2 * tsize, ratio, 2 * lanes)
    right = jnp.asarray(np.ascontiguousarray(right.transpose(1, 0, 2)))
    out_shape = [jax.ShapeDtypeStruct((ratio, window * rows, 2 * lanes), dtype)]
    if fresh:
        out_shape.append(jax.ShapeDtypeStruct((window, tsize, tsize), jnp.bfloat16))
    return pl.pallas_call(
        functools.partial(template_kernel, fresh),
        out_shape=out_shape,
        in_specs=[SMEM] + vmem(3),
        out_specs=vmem(len(out_shape)),
        scratch_shapes=[pltpu.VMEM((window, rows, 2 * tsize), jnp.bfloat16)],
        compiler_params=params(TEMPLATE_MB),
        cost_estimate=pl.CostEstimate(
            flops=2 * window * rows * tsize * (2 * tsize + 4 * win),
            bytes_accessed=2 * bank.size + 4 * window * rows * 2 * win,
            transcendentals=0,
        ),
        name="templates",
    )(orient_index, bank, left, right)


def partial_kernel(count, first, keep_ref, flip_ref, tspec_ref, back_ref, *rest):
    other_refs, rest = rest[:count], rest[count:]
    part_ref, outs = rest[-1], rest[:-1]
    _, _, members, mine, _ = place()
    window = part_ref.shape[0]
    band = keep_ref.shape[0] // 2
    rows = flip_ref.shape[0]
    ratio, _, width = tspec_ref.shape
    lanes = width // 2
    received = jnp.concatenate([other[...] for other in other_refs], 0)
    held = jnp.dot(flip_ref[...], received, preferred_element_type=jnp.float32)
    head = held[:band] + keep_ref[first : first + band]
    held = head if rows == band else jnp.concatenate([head, held[band:]], 0)
    total = None
    for part in range(ratio):
        mic_re = held[:, part * width : part * width + lanes]
        mic_im = held[:, part * width + lanes : (part + 1) * width]
        upper, lower = [], []
        for o in range(window):
            tmpl_re = tspec_ref[part, o * rows : (o + 1) * rows, :lanes].astype(jnp.float32)
            tmpl_im = tspec_ref[part, o * rows : (o + 1) * rows, lanes:].astype(jnp.float32)
            prod_re = mic_re * tmpl_re + mic_im * tmpl_im
            prod_im = mic_im * tmpl_re - mic_re * tmpl_im
            product = jnp.concatenate([prod_re, prod_im], 1)
            rounded = product.astype(jnp.bfloat16)
            upper.append(rounded)
            lower.append((product - rounded.astype(jnp.float32)).astype(jnp.bfloat16))
        upper = jnp.concatenate(upper, 0)
        lower = jnp.concatenate(lower, 0)
        pieces = jnp.concatenate([upper, lower, upper], 1)
        table = jnp.concatenate([back_ref[0, part], back_ref[0, part], back_ref[1, part]], 0)
        got = jnp.dot(pieces, table, preferred_element_type=jnp.float32)
        total = got if total is None else total + got
    for o in range(window):
        part_ref[o] = total[o * rows : (o + 1) * rows]

    group = WCOLS // members
    lane_group = lax.broadcasted_iota(jnp.int32, (rows, WCOLS), 1) // group
    tiles = max(1, window // members)
    for tile in range(tiles):
        for plane in range(2):
            at = slice(plane * WCOLS, (plane + 1) * WCOLS)
            pieces = []
            for i in range(members):
                piece = part_ref[(tile * members + i) % window, :, at]
                pieces.append(pltpu.roll(piece, group * i, 1) if i else piece)
            for s in range(members):
                target = lax.bitwise_xor(mine, s)
                packed = pieces[0]
                for i in range(1, members):
                    inside = (lane_group + (members - i)) % members == target
                    packed = jnp.where(inside, pieces[i], packed)
                start = (plane * tiles + tile) * WCOLS
                outs[s][:, start : start + WCOLS] = packed.astype(outs[s].dtype)


def partials(keep, others, first, flip, tspec, back, members, window):
    rows = flip.shape[0]
    ratio, _, width = tspec.shape
    tiles = max(1, window // members)
    out_shape = (rows, 2 * tiles * WCOLS)
    return pl.pallas_call(
        functools.partial(partial_kernel, len(others), first),
        out_shape=[jax.ShapeDtypeStruct(out_shape, jnp.bfloat16)] * members,
        in_specs=vmem(4 + len(others)),
        out_specs=vmem(members),
        scratch_shapes=[
            pltpu.VMEM((window, rows, 2 * WCOLS), jnp.float32),
        ],
        compiler_params=params(PARTIAL_MB),
        cost_estimate=pl.CostEstimate(
            flops=12 * tspec.size * WCOLS,
            bytes_accessed=2 * tspec.size,
            transcendentals=0,
        ),
        name="partials",
    )(keep, flip, tspec, back, *others)


def column_kernel(group_of, scale, share, roots_ref, *rest):
    row, core, members, mine, side = place()
    cores, classes = lax.axis_size("orient"), lax.axis_size("row")
    many = len(group_of)
    tables, rest = rest[:many], rest[many:]
    low_parts, high_parts = rest[:members], rest[members : 2 * members]
    outs = rest[2 * members : 2 * members + many]
    held_ref, last_ref = rest[2 * members + many :]
    _, steps, depth = tables[0].shape
    low, width = low_parts[0].shape
    band = held_ref.shape[1]
    wide = width // 2
    for s in range(members):
        member = lax.bitwise_xor(mine, s)
        held_ref[member, :low] = low_parts[s][...]
        held_ref[member, low:] = high_parts[s][: band - low]
        last_ref[member] = high_parts[s][band - low :]
    planes = [[], []]
    for member in range(members):
        block = held_ref[member]
        for parity in range(2):
            at = parity * (low // 2)
            piece = jnp.concatenate(
                [block[at : at + low // 2], block[low + at : low + at + low // 2]], 0
            )
            if member and not parity:
                head = piece[:PAD].astype(jnp.float32) + last_ref[member - 1].astype(jnp.float32)
                piece = jnp.concatenate([head.astype(jnp.bfloat16), piece[PAD:]], 0)
            planes[parity].append((piece[:, :wide], piece[:, wide:]))
    top = last_ref[members - 1][:1, :wide].astype(jnp.float32)
    group = WCOLS // members
    height = steps // (members // 2)
    lane_group = lax.broadcasted_iota(jnp.int32, (height, WCOLS), 1) // group
    kappa = (lane_group + (members - mine)) % members
    for which in range(many):
        rho = reverse_bits(lax.bitwise_xor(row, group_of[which]), bits(classes))
        sums = [(1 - 2 * (rho % 2)).astype(jnp.float32) * top, 0.0]
        for parity in range(2):
            for turn in range(members // cores):
                angle = rho * turn % classes
                cos = roots_ref[0, angle].astype(jnp.bfloat16)
                sin = roots_ref[1, angle].astype(jnp.bfloat16)
                blocks = []
                for re, im in planes[parity][turn * cores : (turn + 1) * cores]:
                    blocks += [cos * re - sin * im, sin * re + cos * im] if turn else [re, im]
                stacked = jnp.concatenate(blocks, 0)
                got = jnp.dot(tables[which][parity], stacked, preferred_element_type=jnp.float32)
                sums[parity] = sums[parity] + got[: steps // 2] + got[steps // 2 :]
        corr = jnp.concatenate([sums[0] + sums[1], sums[0] - sums[1]], 0)
        corr = corr * (scale * (1 - 2 * (side * rho % 2)).astype(jnp.float32))
        peak = corr[:, :WCOLS]
        power = corr[:, :WCOLS] * corr[:, :WCOLS]
        for start in range(WCOLS, wide, WCOLS):
            more = corr[:, start : start + WCOLS]
            peak = jnp.maximum(peak, more)
            power = power + more * more
        shift = group
        while shift < WCOLS:
            peak = jnp.maximum(peak, pltpu.roll(peak, shift, 1))
            power = power + pltpu.roll(power, shift, 1)
            shift *= 2
        if share != 1.0:
            power = power * share
        packed = peak[:height]
        for k in range(1, members):
            source = (power if k % 2 else peak)[k // 2 * height : (k // 2 + 1) * height]
            packed = jnp.where(kappa == k, source, packed)
        outs[which][...] = packed.astype(outs[which].dtype)


def columns(parts, tables, group_of, classes, band, scale, share, dtype):
    members = len(parts) // 2
    many = len(group_of)
    steps = tables[0].shape[1]
    height = steps // (members // 2)
    width = parts[0].shape[1]
    roots = np.round(np.exp(2j * np.pi * np.arange(classes) / classes), 12)
    roots = jnp.asarray(np.stack([roots.real, roots.imag]).astype(np.float32))
    return pl.pallas_call(
        functools.partial(column_kernel, group_of, scale, share),
        out_shape=[jax.ShapeDtypeStruct((height, WCOLS), dtype)] * many,
        in_specs=[SMEM] + vmem(many + 2 * members),
        out_specs=vmem(many),
        scratch_shapes=[
            pltpu.VMEM((members, band, width), jnp.bfloat16),
            pltpu.VMEM((members, PAD, width), jnp.bfloat16),
        ],
        compiler_params=params(COLUMN_MB),
        cost_estimate=pl.CostEstimate(
            flops=many * 2 * tables[0].size * width // 2,
            bytes_accessed=2 * many * tables[0].size,
            transcendentals=0,
        ),
        name="columns",
    )(roots, *tables, *parts)


def unpack_kernel(classes, *rest):
    near = rest[:classes]
    far = rest[classes : 2 * classes]
    peak_ref, power_ref = rest[2 * classes :]
    row, core, members, _, side = place()
    half = classes // 2
    height = near[0].shape[0]
    group = WCOLS // members
    lane_group = lax.broadcasted_iota(jnp.int32, (height, WCOLS), 1) // group
    for delta in range(2):
        mic = lax.bitwise_xor(side, delta)
        for k in range(members):
            wanted = (lane_group + (members - k)) % members
            value = jnp.zeros((height, WCOLS), jnp.float32)
            for low in range(half):
                s = delta * half + low
                base = lax.bitwise_xor(row, s) % half * 2
                for source, at in ((near, core), (far, 1 - core)):
                    value = jnp.where(wanted == base + at, source[s][...].astype(jnp.float32), value)
            if k:
                value = pltpu.roll(value, WCOLS - k * group, 1)
            target = power_ref if k % 2 else peak_ref
            target[mic, 0, k // 2 * height : (k // 2 + 1) * height, :] = value


def unpack(near, far, steps):
    classes = len(near)
    shape = jax.ShapeDtypeStruct((2, 1, steps, WCOLS), jnp.float32)
    return pl.pallas_call(
        functools.partial(unpack_kernel, classes),
        out_shape=[shape, shape],
        in_specs=vmem(2 * classes),
        out_specs=vmem(2),
        compiler_params=params(8),
        name="unpack",
    )(*near, *far)


def shards(spectra, bank, orient_index):
    length = spectra.shape[3]
    tsize = bank.shape[1]
    classes = lax.axis_size("row")
    cores = lax.axis_size("orient")
    count = classes * cores
    members = count // 2
    band = length // count
    steps = length // classes
    win = 1 << (tsize + WCOLS - 2).bit_length()
    lanes = win // (length // win)
    line = ("row", "orient")
    window = orient_index.shape[0]
    rows = band // 2

    row = lax.axis_index("row")
    window_tables = jnp.asarray(
        np.stack([window_table(length, win, True), window_table(length, win, False)])
    )
    back = jnp.asarray(back_table(win, lanes))
    flip = flip_table(band)
    order = sorted_rows(rows)
    flips = [flip[:rows, rows:][order], np.concatenate([flip[rows:band][order], flip[band:]], 0)]

    opposite = [(i, count - 1 - i) for i in range(count)]
    cos, sin = phases(np.arange(length + PAD), np.arange(tsize), length)
    left = np.stack([cos, -sin]).astype(BF16)
    chunked = left[:, :length].reshape(2, -1, rows, tsize)[:, :, sorted_rows(rows)]
    left = jnp.asarray(np.concatenate([chunked.reshape(2, length, tsize), left[:, length:]], 1))
    sent = window_first(spectra, window_tables, rows)
    others = [lax.ppermute(sent, line, opposite)]
    spectra, bank, _ = lax.optimization_barrier((spectra, bank, sent))
    sent, keep, *left = window_rest(spectra, window_tables, left, rows)
    others.insert(0, lax.ppermute(sent, line, opposite))
    bank, keep, *left = lax.optimization_barrier((bank, keep, *left))
    lows, highs = [], []
    for block, got in ((0, lows), (1, highs)):
        tspec, *fresh = template_spectra(
            bank, orient_index, left[block], win, lanes, jnp.float32, block == 0
        )
        parts = partials(
            keep,
            others[1 - block :],
            block * rows,
            jnp.asarray(flips[block]),
            tspec,
            back,
            members,
            window,
        )
        got.append(parts[0])
        for s in range(1, members):
            got.append(lax.ppermute(parts[s], line, [(i, i ^ s) for i in range(count)]))
        if block == 0:
            bank, left[1], _ = lax.optimization_barrier((fresh[0], left[1], parts[0]))
            early = lows[1 : members // 2 + 1]
            others[0], *early = lax.optimization_barrier((others[0], *early))
            lows[1 : members // 2 + 1] = early

    all_tables = jnp.asarray(column_table(length, classes, cores, band))
    row, _ = lax.optimization_barrier((row, parts[0]))
    maps = [None] * classes
    for group in (range(classes // 2, classes), range(classes // 2)):
        rhos = [reverse_bits(lax.bitwise_xor(row, s), bits(classes)) for s in group]
        made = columns(
            lows + highs,
            [lax.dynamic_index_in_dim(all_tables, rho, 0, False) for rho in rhos],
            tuple(group),
            classes,
            band,
            1.0 / (length * tsize),
            window / max(window, members),
            jnp.bfloat16,
        )
        for s, one in zip(group, made):
            maps[s] = one
    near = [maps[0]]
    for s in range(1, classes):
        near.append(lax.ppermute(maps[s], "row", [(i, i ^ s) for i in range(classes)]))
    far = [lax.ppermute(m, "orient", [(0, 1), (1, 0)]) for m in near]
    peak, power = unpack(near, far, steps)
    return peak, power


def solution(mesh):
    return jax.shard_map(
        shards,
        mesh=mesh,
        in_specs=(P(("grp", "mic"), None, "row", None), P(), P("grp")),
        out_specs=(P(("grp", "mic"), "row", None, None), P(("grp", "mic"), "row", None, None)),
        check_vma=False,
    )
```

```python
import functools
import math

import jax
import jax.numpy as jnp
import ml_dtypes
import numpy as np
from jax import lax
from jax.experimental import pallas as pl
from jax.experimental.pallas import tpu as pltpu
from jax.sharding import PartitionSpec as P

WCOLS = 128
WINDOW_MB = 57
TEMPLATE_MB = 16
PARTIAL_MB = 16
COLUMN_MB = 12
PAD = 16

two_pi = 2.0 * math.pi
BF16 = ml_dtypes.bfloat16


def params(mebibytes):
    return pltpu.CompilerParams(vmem_limit_bytes=mebibytes * 1024 * 1024)


def bits(count):
    return count.bit_length() - 1


def reverse_bits(number, digits):
    result = number * 0
    for digit in range(digits):
        result = result + number // (1 << digit) % 2 * (1 << digits - 1 - digit)
    return result


def phases(rows, cols, period):
    angles = np.outer(rows, cols) % period * (two_pi / period)
    return np.cos(angles), np.sin(angles)


def window_table(length, win, mirrored):
    ratio = length // win
    lanes = win // ratio
    sign = 1 if mirrored else -1
    base = np.arange(win)[:, None] + sign * ratio * np.arange(lanes)[None, :]
    d = (length // ratio * np.arange(ratio)[:, None, None] + base[None]) % length
    u = np.arange(win)
    kernel = np.exp(2j * np.pi * (np.outer(np.arange(length), u) % length) / length).sum(1) / win
    val = kernel[d]
    return np.concatenate([val.real, val.imag], 2).astype(BF16)


def tiles_of(re, im, lanes, axis):
    pieces = []
    for start in range(0, re.shape[axis], lanes):
        cut = [slice(None)] * re.ndim
        cut[axis] = slice(start, start + lanes)
        pieces += [re[tuple(cut)], im[tuple(cut)]]
    return np.concatenate(pieces, axis)


def template_table(tsize, win, lanes):
    cos, sin = phases(np.arange(tsize), np.arange(win), win)
    upper = tiles_of(cos, -sin, lanes, 1)
    lower = tiles_of(sin, cos, lanes, 1)
    return np.concatenate([upper, lower], 0).astype(BF16)


def split(table):
    upper = table.astype(BF16)
    return np.stack([upper, (table - upper.astype(np.float64)).astype(BF16)])


def back_table(win, lanes):
    cos, sin = phases(np.arange(win), np.arange(WCOLS), win)
    re_rows = np.concatenate([cos, sin], 1)
    im_rows = np.concatenate([-sin, cos], 1)
    table = tiles_of(re_rows, im_rows, lanes, 0)
    return split(table.reshape(win // lanes, 2 * lanes, 2 * WCOLS))


def sorted_rows(count):
    return np.concatenate([np.arange(0, count, 2), np.arange(1, count, 2)])


def column_table(length, classes, cores, band):
    steps = length // classes
    freqs = np.arange(cores * band)
    out = []
    for rho in range(classes):
        rows = rho + classes * np.arange(steps // 2)
        for parity in range(2):
            cos, sin = phases(rows, freqs[parity::2], length)
            upper, lower = split(tiles_of(cos, -sin, band // 2, 1))
            out.append(np.concatenate([upper, lower], 0))
    return np.stack(out).reshape(classes, 2, steps, cores * band)


def flip_table(band):
    out = np.zeros((band + PAD, band), np.float32)
    out[band - np.arange(band), np.arange(band)] = 1.0
    return out.astype(BF16)


def vmem(count):
    return [pl.BlockSpec(memory_space=pltpu.VMEM)] * count


def hbm(count):
    return [pl.BlockSpec(memory_space=pltpu.HBM)] * count


SMEM = pl.BlockSpec(memory_space=pltpu.SMEM)


def place():
    row, core = lax.axis_index("row"), lax.axis_index("orient")
    cores = lax.axis_size("orient")
    members = lax.axis_size("row") * cores // 2
    device = row * cores + core
    return row, core, members, device % members, device // members


def window_block(mirrored, spec, table, out_ref, order=None):
    rows, total = out_ref.shape
    ratio = table(None)
    width = total // ratio
    lanes = width // 2
    win = ratio * lanes
    pieces = []
    for step in range(ratio):
        at = slice(step * win, (step + 1) * win)
        pieces += [spec(part, at) for part in range(2)]
    stacked = jnp.concatenate(pieces, 0)
    got = [
        jnp.dot(stacked, table(which), preferred_element_type=jnp.float32)
        for which in range(ratio)
    ]
    for part in range(ratio):
        re, im = 0.0, 0.0
        for which in range(ratio):
            step = (which - part if mirrored else which + part) % ratio
            re = re + got[which][2 * step * rows : (2 * step + 1) * rows]
            im = im + got[which][(2 * step + 1) * rows : (2 * step + 2) * rows]
        out_re = re[:, :lanes] - im[:, lanes:]
        out_im = re[:, lanes:] + im[:, :lanes]
        if mirrored:
            out_im = -out_im
        both = jnp.concatenate([out_re, out_im], 1)
        if order is not None:
            upper = both.astype(jnp.bfloat16)
            lower = (both - upper.astype(jnp.float32)).astype(jnp.bfloat16)
            both = jnp.dot(order, upper, preferred_element_type=jnp.float32)
            both += jnp.dot(order, lower, preferred_element_type=jnp.float32)
        out_ref[:, part * width : (part + 1) * width] = both.astype(out_ref.dtype)


def first_kernel(spec_ref, tables_ref, out_ref, held_ref, table_ref, sem):
    rows = out_ref.shape[0]
    _, core, _, _, side = place()
    start = pl.multiple_of((2 * core + 1) * rows, rows)
    copies = [
        pltpu.make_async_copy(
            spec_ref.at[1 - side, :, pl.ds(start, rows)], held_ref, sem.at[0]
        ),
        pltpu.make_async_copy(tables_ref.at[0], table_ref, sem.at[1]),
    ]
    for copy in copies:
        copy.start()
    for copy in copies:
        copy.wait()
    window_block(
        True,
        lambda part, at: held_ref[part, :, at],
        lambda k: table_ref.shape[0] if k is None else table_ref[k],
        out_ref,
    )


def window_first(spectra, tables, rows):
    _, ratio, win, width = tables.shape
    return pl.pallas_call(
        first_kernel,
        out_shape=jax.ShapeDtypeStruct((rows, ratio * width), jnp.bfloat16),
        in_specs=hbm(2),
        out_specs=vmem(1)[0],
        scratch_shapes=[
            pltpu.VMEM((2, rows, ratio * win), jnp.bfloat16),
            pltpu.VMEM((ratio, win, width), jnp.bfloat16),
            pltpu.SemaphoreType.DMA((2,)),
        ],
        compiler_params=params(WINDOW_MB),
        cost_estimate=pl.CostEstimate(
            flops=4 * rows * ratio * win * ratio * width,
            bytes_accessed=8 * rows * ratio * win,
            transcendentals=0,
        ),
        name="window_first",
    )(spectra, tables)


def rest_kernel(place_ref, spec_ref, table_ref, order_ref, main_ref, more_ref, *outs):
    sent_ref, keep_ref, low_ref, high_ref = outs
    step = pl.program_id(0)
    spec = lambda part, at: spec_ref[0, part, :, at]
    table = lambda k: table_ref.shape[1] if k is None else table_ref[0, k]

    @pl.when(step == 0)
    def _():
        window_block(True, spec, table, sent_ref)
        low, band = low_ref.shape[1], main_ref.shape[1]
        low_ref[...] = main_ref[:, :low]
        high_ref[:, : band - low] = main_ref[:, low:]
        high_ref[:, band - low :] = more_ref[...]

    @pl.when(step > 0)
    def _():
        window_block(False, spec, table, keep_ref, order_ref[...])


def window_rest(spectra, tables, left, rows):
    _, ratio, win, width = tables.shape
    row, core, members, _, side = place()
    device = row * lax.axis_size("orient") + core
    band = 2 * rows
    tsize = left.shape[2]
    at = jnp.stack([side, core, device]).astype(jnp.int32)
    order = jnp.asarray(np.eye(rows)[sorted_rows(rows)].astype(BF16))

    def spec_index(i, at):
        first = jnp.where(i == 0, 1, 0)
        return at[0] + first * (1 - 2 * at[0]), 0, 2 * at[1] + jnp.maximum(i - 1, 0), 0

    return pl.pallas_call(
        rest_kernel,
        out_shape=[
            jax.ShapeDtypeStruct((rows, ratio * width), jnp.bfloat16),
            jax.ShapeDtypeStruct((band, ratio * width), jnp.float32),
            jax.ShapeDtypeStruct((2, rows, tsize), jnp.bfloat16),
            jax.ShapeDtypeStruct((2, rows + PAD, tsize), jnp.bfloat16),
        ],
        grid_spec=pltpu.PrefetchScalarGridSpec(
            num_scalar_prefetch=1,
            grid=(3,),
            in_specs=[
                pl.BlockSpec((1, 2, rows, ratio * win), spec_index),
                pl.BlockSpec((1, ratio, win, width), lambda i, at: (jnp.minimum(i, 1), 0, 0, 0)),
                pl.BlockSpec((rows, rows), lambda i, at: (0, 0)),
                pl.BlockSpec((2, band, tsize), lambda i, at: (0, at[2], 0)),
                pl.BlockSpec((2, PAD, tsize), lambda i, at: (0, (at[2] + 1) * (band // PAD), 0)),
            ],
            out_specs=[
                pl.BlockSpec((rows, ratio * width), lambda i, at: (0, 0)),
                pl.BlockSpec((rows, ratio * width), lambda i, at: (jnp.maximum(i - 1, 0), 0)),
                pl.BlockSpec((2, rows, tsize), lambda i, at: (0, 0, 0)),
                pl.BlockSpec((2, rows + PAD, tsize), lambda i, at: (0, 0, 0)),
            ],
        ),
        compiler_params=params(WINDOW_MB),
        cost_estimate=pl.CostEstimate(
            flops=12 * rows * ratio * win * ratio * width,
            bytes_accessed=20 * rows * ratio * win,
            transcendentals=0,
        ),
        name="window_rest",
    )(at, spectra, tables, order, left, left)


def template_kernel(fresh, index_ref, bank_ref, left_ref, right_ref, out_ref, *rest):
    hold_ref = rest[-1]
    ratio, depth, width = right_ref.shape
    window, rows = hold_ref.shape[0], hold_ref.shape[1]
    left = jnp.concatenate([left_ref[0], left_ref[1]], 0)
    for o in range(window):
        if fresh:
            values = bank_ref[index_ref[o]].astype(jnp.float32)
            share = 1.0 / values.size
            total = jnp.sum(jnp.sum(values, 0, keepdims=True), 1, keepdims=True)
            centred = values - total * share
            square = jnp.sum(jnp.sum(centred * centred, 0, keepdims=True), 1, keepdims=True)
            factor = lax.rsqrt(square * share + 1e-06)
            template = (centred * factor).astype(jnp.bfloat16)
            rest[0][o] = template
        else:
            template = bank_ref[o]
        rowpass = jnp.dot(left, template, preferred_element_type=jnp.float32).astype(jnp.bfloat16)
        hold_ref[o] = jnp.concatenate([rowpass[:rows], rowpass[rows:]], 1)
    flat = hold_ref[...].reshape(window * rows, depth)
    for part in range(ratio):
        got = jnp.dot(flat, right_ref[part], preferred_element_type=jnp.float32)
        out_ref[part] = got.astype(out_ref.dtype)


def template_spectra(bank, orient_index, left, win, lanes, dtype, fresh):
    tsize = bank.shape[1]
    window = orient_index.shape[0]
    ratio = win // lanes
    rows = left.shape[1]
    right = template_table(tsize, win, lanes).reshape(2 * tsize, ratio, 2 * lanes)
    right = jnp.asarray(np.ascontiguousarray(right.transpose(1, 0, 2)))
    out_shape = [jax.ShapeDtypeStruct((ratio, window * rows, 2 * lanes), dtype)]
    if fresh:
        out_shape.append(jax.ShapeDtypeStruct((window, tsize, tsize), jnp.bfloat16))
    return pl.pallas_call(
        functools.partial(template_kernel, fresh),
        out_shape=out_shape,
        in_specs=[SMEM] + vmem(3),
        out_specs=vmem(len(out_shape)),
        scratch_shapes=[pltpu.VMEM((window, rows, 2 * tsize), jnp.bfloat16)],
        compiler_params=params(TEMPLATE_MB),
        cost_estimate=pl.CostEstimate(
            flops=2 * window * rows * tsize * (2 * tsize + 4 * win),
            bytes_accessed=2 * bank.size + 4 * window * rows * 2 * win,
            transcendentals=0,
        ),
        name="templates",
    )(orient_index, bank, left, right)


def partial_kernel(count, first, keep_ref, flip_ref, tspec_ref, back_ref, *rest):
    other_refs, rest = rest[:count], rest[count:]
    part_ref, outs = rest[-1], rest[:-1]
    _, _, members, mine, _ = place()
    window = part_ref.shape[0]
    band = keep_ref.shape[0] // 2
    rows = flip_ref.shape[0]
    ratio, _, width = tspec_ref.shape
    lanes = width // 2
    received = jnp.concatenate([other[...] for other in other_refs], 0)
    held = jnp.dot(flip_ref[...], received, preferred_element_type=jnp.float32)
    head = held[:band] + keep_ref[first : first + band]
    held = head if rows == band else jnp.concatenate([head, held[band:]], 0)
    total = None
    for part in range(ratio):
        mic_re = held[:, part * width : part * width + lanes]
        mic_im = held[:, part * width + lanes : (part + 1) * width]
        upper, lower = [], []
        for o in range(window):
            tmpl_re = tspec_ref[part, o * rows : (o + 1) * rows, :lanes].astype(jnp.float32)
            tmpl_im = tspec_ref[part, o * rows : (o + 1) * rows, lanes:].astype(jnp.float32)
            prod_re = mic_re * tmpl_re + mic_im * tmpl_im
            prod_im = mic_im * tmpl_re - mic_re * tmpl_im
            product = jnp.concatenate([prod_re, prod_im], 1)
            rounded = product.astype(jnp.bfloat16)
            upper.append(rounded)
            lower.append((product - rounded.astype(jnp.float32)).astype(jnp.bfloat16))
        upper = jnp.concatenate(upper, 0)
        lower = jnp.concatenate(lower, 0)
        pieces = jnp.concatenate([upper, lower, upper], 1)
        table = jnp.concatenate([back_ref[0, part], back_ref[0, part], back_ref[1, part]], 0)
        got = jnp.dot(pieces, table, preferred_element_type=jnp.float32)
        total = got if total is None else total + got
    for o in range(window):
        part_ref[o] = total[o * rows : (o + 1) * rows]

    group = WCOLS // members
    lane_group = lax.broadcasted_iota(jnp.int32, (rows, WCOLS), 1) // group
    tiles = max(1, window // members)
    for tile in range(tiles):
        for plane in range(2):
            at = slice(plane * WCOLS, (plane + 1) * WCOLS)
            pieces = []
            for i in range(members):
                piece = part_ref[(tile * members + i) % window, :, at]
                pieces.append(pltpu.roll(piece, group * i, 1) if i else piece)
            for s in range(members):
                target = lax.bitwise_xor(mine, s)
                packed = pieces[0]
                for i in range(1, members):
                    inside = (lane_group + (members - i)) % members == target
                    packed = jnp.where(inside, pieces[i], packed)
                start = (plane * tiles + tile) * WCOLS
                outs[s][:, start : start + WCOLS] = packed.astype(outs[s].dtype)


def partials(keep, others, first, flip, tspec, back, members, window):
    rows = flip.shape[0]
    ratio, _, width = tspec.shape
    tiles = max(1, window // members)
    out_shape = (rows, 2 * tiles * WCOLS)
    return pl.pallas_call(
        functools.partial(partial_kernel, len(others), first),
        out_shape=[jax.ShapeDtypeStruct(out_shape, jnp.bfloat16)] * members,
        in_specs=vmem(4 + len(others)),
        out_specs=vmem(members),
        scratch_shapes=[
            pltpu.VMEM((window, rows, 2 * WCOLS), jnp.float32),
        ],
        compiler_params=params(PARTIAL_MB),
        cost_estimate=pl.CostEstimate(
            flops=12 * tspec.size * WCOLS,
            bytes_accessed=2 * tspec.size,
            transcendentals=0,
        ),
        name="partials",
    )(keep, flip, tspec, back, *others)


def column_kernel(group_of, scale, share, roots_ref, *rest):
    row, core, members, mine, side = place()
    cores, classes = lax.axis_size("orient"), lax.axis_size("row")
    many = len(group_of)
    tables, rest = rest[:many], rest[many:]
    low_parts, high_parts = rest[:members], rest[members : 2 * members]
    outs = rest[2 * members : 2 * members + many]
    held_ref, last_ref = rest[2 * members + many :]
    _, steps, depth = tables[0].shape
    low, width = low_parts[0].shape
    band = held_ref.shape[1]
    wide = width // 2
    for s in range(members):
        member = lax.bitwise_xor(mine, s)
        held_ref[member, :low] = low_parts[s][...]
        held_ref[member, low:] = high_parts[s][: band - low]
        last_ref[member] = high_parts[s][band - low :]
    planes = [[], []]
    for member in range(members):
        block = held_ref[member]
        for parity in range(2):
            at = parity * (low // 2)
            piece = jnp.concatenate(
                [block[at : at + low // 2], block[low + at : low + at + low // 2]], 0
            )
            if member and not parity:
                head = piece[:PAD].astype(jnp.float32) + last_ref[member - 1].astype(jnp.float32)
                piece = jnp.concatenate([head.astype(jnp.bfloat16), piece[PAD:]], 0)
            planes[parity].append((piece[:, :wide], piece[:, wide:]))
    top = last_ref[members - 1][:1, :wide].astype(jnp.float32)
    group = WCOLS // members
    height = steps // (members // 2)
    lane_group = lax.broadcasted_iota(jnp.int32, (height, WCOLS), 1) // group
    kappa = (lane_group + (members - mine)) % members
    for which in range(many):
        rho = reverse_bits(lax.bitwise_xor(row, group_of[which]), bits(classes))
        sums = [(1 - 2 * (rho % 2)).astype(jnp.float32) * top, 0.0]
        for parity in range(2):
            blocks = []
            for turn in range(members // cores):
                angle = rho * turn % classes
                cos = roots_ref[0, angle].astype(jnp.bfloat16)
                sin = roots_ref[1, angle].astype(jnp.bfloat16)
                for re, im in planes[parity][turn * cores : (turn + 1) * cores]:
                    blocks += [cos * re - sin * im, sin * re + cos * im] if turn else [re, im]
            table = jnp.concatenate([tables[which][parity]] * (members // cores), 1)
            stacked = jnp.concatenate(blocks, 0)
            got = jnp.dot(table, stacked, preferred_element_type=jnp.float32)
            sums[parity] = sums[parity] + got[: steps // 2] + got[steps // 2 :]
        corr = jnp.concatenate([sums[0] + sums[1], sums[0] - sums[1]], 0)
        corr = corr * (scale * (1 - 2 * (side * rho % 2)).astype(jnp.float32))
        peak = corr[:, :WCOLS]
        power = corr[:, :WCOLS] * corr[:, :WCOLS]
        for start in range(WCOLS, wide, WCOLS):
            more = corr[:, start : start + WCOLS]
            peak = jnp.maximum(peak, more)
            power = power + more * more
        shift = group
        while shift < WCOLS:
            peak = jnp.maximum(peak, pltpu.roll(peak, shift, 1))
            power = power + pltpu.roll(power, shift, 1)
            shift *= 2
        if share != 1.0:
            power = power * share
        packed = peak[:height]
        for k in range(1, members):
            source = (power if k % 2 else peak)[k // 2 * height : (k // 2 + 1) * height]
            packed = jnp.where(kappa == k, source, packed)
        outs[which][...] = packed.astype(outs[which].dtype)


def columns(parts, tables, group_of, classes, band, scale, share, dtype):
    members = len(parts) // 2
    many = len(group_of)
    steps = tables[0].shape[1]
    height = steps // (members // 2)
    width = parts[0].shape[1]
    roots = np.round(np.exp(2j * np.pi * np.arange(classes) / classes), 12)
    roots = jnp.asarray(np.stack([roots.real, roots.imag]).astype(np.float32))
    return pl.pallas_call(
        functools.partial(column_kernel, group_of, scale, share),
        out_shape=[jax.ShapeDtypeStruct((height, WCOLS), dtype)] * many,
        in_specs=[SMEM] + vmem(many + 2 * members),
        out_specs=vmem(many),
        scratch_shapes=[
            pltpu.VMEM((members, band, width), jnp.bfloat16),
            pltpu.VMEM((members, PAD, width), jnp.bfloat16),
        ],
        compiler_params=params(COLUMN_MB),
        cost_estimate=pl.CostEstimate(
            flops=many * 2 * tables[0].size * width // 2,
            bytes_accessed=2 * many * tables[0].size,
            transcendentals=0,
        ),
        name="columns",
    )(roots, *tables, *parts)


def unpack_kernel(classes, *rest):
    near = rest[:classes]
    far = rest[classes : 2 * classes]
    peak_ref, power_ref = rest[2 * classes :]
    row, core, members, _, side = place()
    half = classes // 2
    height = near[0].shape[0]
    group = WCOLS // members
    lane_group = lax.broadcasted_iota(jnp.int32, (height, WCOLS), 1) // group
    for delta in range(2):
        mic = lax.bitwise_xor(side, delta)
        for k in range(members):
            wanted = (lane_group + (members - k)) % members
            value = jnp.zeros((height, WCOLS), jnp.float32)
            for low in range(half):
                s = delta * half + low
                base = lax.bitwise_xor(row, s) % half * 2
                for source, at in ((near, core), (far, 1 - core)):
                    value = jnp.where(wanted == base + at, source[s][...].astype(jnp.float32), value)
            if k:
                value = pltpu.roll(value, WCOLS - k * group, 1)
            target = power_ref if k % 2 else peak_ref
            target[mic, 0, k // 2 * height : (k // 2 + 1) * height, :] = value


def unpack(near, far, steps):
    classes = len(near)
    shape = jax.ShapeDtypeStruct((2, 1, steps, WCOLS), jnp.float32)
    return pl.pallas_call(
        functools.partial(unpack_kernel, classes),
        out_shape=[shape, shape],
        in_specs=vmem(2 * classes),
        out_specs=vmem(2),
        compiler_params=params(8),
        name="unpack",
    )(*near, *far)


def shards(spectra, bank, orient_index):
    length = spectra.shape[3]
    tsize = bank.shape[1]
    classes = lax.axis_size("row")
    cores = lax.axis_size("orient")
    count = classes * cores
    members = count // 2
    band = length // count
    steps = length // classes
    win = 1 << (tsize + WCOLS - 2).bit_length()
    lanes = win // (length // win)
    line = ("row", "orient")
    window = orient_index.shape[0]
    rows = band // 2

    row = lax.axis_index("row")
    window_tables = jnp.asarray(
        np.stack([window_table(length, win, True), window_table(length, win, False)])
    )
    back = jnp.asarray(back_table(win, lanes))
    flip = flip_table(band)
    order = sorted_rows(rows)
    flips = [flip[:rows, rows:][order], np.concatenate([flip[rows:band][order], flip[band:]], 0)]

    opposite = [(i, count - 1 - i) for i in range(count)]
    cos, sin = phases(np.arange(length + PAD), np.arange(tsize), length)
    left = np.stack([cos, -sin]).astype(BF16)
    chunked = left[:, :length].reshape(2, -1, rows, tsize)[:, :, sorted_rows(rows)]
    left = jnp.asarray(np.concatenate([chunked.reshape(2, length, tsize), left[:, length:]], 1))
    sent = window_first(spectra, window_tables, rows)
    others = [lax.ppermute(sent, line, opposite)]
    spectra, bank, _ = lax.optimization_barrier((spectra, bank, sent))
    sent, keep, *left = window_rest(spectra, window_tables, left, rows)
    others.insert(0, lax.ppermute(sent, line, opposite))
    bank, keep, *left = lax.optimization_barrier((bank, keep, *left))
    lows, highs = [], []
    for block, got in ((0, lows), (1, highs)):
        tspec, *fresh = template_spectra(
            bank, orient_index, left[block], win, lanes, jnp.float32, block == 0
        )
        parts = partials(
            keep,
            others[1 - block :],
            block * rows,
            jnp.asarray(flips[block]),
            tspec,
            back,
            members,
            window,
        )
        got.append(parts[0])
        for s in range(1, members):
            got.append(lax.ppermute(parts[s], line, [(i, i ^ s) for i in range(count)]))
        if block == 0:
            bank, left[1], _ = lax.optimization_barrier((fresh[0], left[1], parts[0]))
            early = lows[1 : members // 2 + 1]
            others[0], *early = lax.optimization_barrier((others[0], *early))
            lows[1 : members // 2 + 1] = early

    all_tables = jnp.asarray(column_table(length, classes, cores, band))
    row, _ = lax.optimization_barrier((row, parts[0]))
    maps = [None] * classes
    for group in (range(classes // 2, classes), range(classes // 2)):
        rhos = [reverse_bits(lax.bitwise_xor(row, s), bits(classes)) for s in group]
        made = columns(
            lows + highs,
            [lax.dynamic_index_in_dim(all_tables, rho, 0, False) for rho in rhos],
            tuple(group),
            classes,
            band,
            1.0 / (length * tsize),
            window / max(window, members),
            jnp.bfloat16,
        )
        for s, one in zip(group, made):
            maps[s] = one
    near = [maps[0]]
    for s in range(1, classes):
        near.append(lax.ppermute(maps[s], "row", [(i, i ^ s) for i in range(classes)]))
    far = [lax.ppermute(m, "orient", [(0, 1), (1, 0)]) for m in near]
    peak, power = unpack(near, far, steps)
    return peak, power


def solution(mesh):
    return jax.shard_map(
        shards,
        mesh=mesh,
        in_specs=(P(("grp", "mic"), None, "row", None), P(), P("grp")),
        out_specs=(P(("grp", "mic"), "row", None, None), P(("grp", "mic"), "row", None, None)),
        check_vma=False,
    )
```
